512 devices in a mesh: dp: 64 (over y, z_lo, core), tensor: 8 (over z_hi, x).
Axes of the slice: x: 4, y: 8, z: 8 (z_hi: 2, z_lo: 4; z = z_hi * 4 + z_lo), core: 2. Of those that a mesh axis runs over, the one named last changes fastest.
Arguments:
- acts: bfloat16 [65536, 7168], P('dp', 'tensor'), may hold values from -6 to 6
- targets: bfloat16 [65536, 384], P('dp'), may hold values from -6 to 6
- probe: int32 [7168, 384], P('tensor'), may hold values from 0 to 1
- master: float32 [7168, 384], P(('tensor', 'dp')), may hold values from -0.28347334 to 0.28347334
- moment: float32 [7168, 384], P(('tensor', 'dp')), may hold values from -0.6 to 0.6
- curv: float32 [7168, 384], P(('tensor', 'dp')), may hold values from 0.05 to 2
Outputs:
- new_weight: bfloat16 [7168, 384], P('tensor')
- moment_out: float32 [7168, 384], P(('tensor', 'dp'))
- curv_out: float32 [7168, 384], P(('tensor', 'dp'))
The draws below stay inside these ranges and needn't reach their ends.
All inputs are finite; a program needn't handle non-finite values.
Results may differ from the reference program's by a relative error of at most 0.0053.
Values may be sent and summed in bfloat16 or wider, within the bound.
A program may use at most 64 MiB of HBM per device.

```python
import math
import jax
import jax.numpy as jnp

D = 7168
COLS = 384
TOKENS = 65536


def touch_ends(values, stream_key, least, top_value):
    longest = values.shape.index(max(values.shape))
    spots = []
    for shift in (0, 1):
        where = [jax.random.randint(jax.random.fold_in(stream_key, axis), (), 0, length) for axis, length in enumerate(values.shape)]
        where[longest] = (where[longest] + shift) % values.shape[longest]
        spots.append(tuple(where))
    return values.at[spots[0]].set(least).at[spots[1]].set(top_value)


def spiked(drawn, own_key, source, target, parts, factor):
    def block_of(axis_at):
        return (jnp.arange(drawn.shape[axis_at]) // (drawn.shape[axis_at] // parts)).reshape((-1,) + (1,) * (drawn.ndim - 1 - axis_at))

    near = jax.random.permutation(own_key, parts)[block_of(target)]
    far = (block_of(target) + parts // 2) % parts
    return jnp.where((block_of(source) == near) | (block_of(source) == far), factor * drawn, drawn)


def block_levels(own_key, dims, shards, low, largest):
    factor_of, own = 1.0, jax.random.fold_in(own_key, 6)
    for dim, shards_of in shards:
        heights = jnp.exp(jax.random.uniform(jax.random.fold_in(own, dim), (shards_of,), jnp.float32, low / len(shards), largest / len(shards)))
        factor_of = factor_of * jnp.repeat(heights, dims[dim] // shards_of).reshape([-1 if axis == dim else 1 for axis in range(len(dims))])
    return factor_of


def bell_draw(stream_key, extent, deviation, bound, split=(), held_as=jnp.bfloat16):
    entries = jax.random.normal(stream_key, extent, jnp.float32) * deviation
    if len(split) > 0:
        entries = block_levels(stream_key, extent, split, -0.22, 0.18) * entries
    return jnp.clip(entries, min=-bound, max=bound).astype(held_as)


def gaussian_with(stream_key, dims, scale, limit, shards, heavy, held_as=jnp.bfloat16):
    result = scale * jax.random.normal(stream_key, dims, jnp.float32)
    if shards:
        result = result * block_levels(stream_key, dims, shards, -0.22, 0.18)
    return jnp.clip(spiked(result, jax.random.fold_in(stream_key, 3), *heavy), -limit, limit).astype(held_as)


def setup_inputs(seed: int = 0) -> dict:
    splits = jax.random.split(jax.random.key(seed), 7)
    acts = gaussian_with(splits[0], (TOKENS, D), 0.35, 6.0, ((0, 64), (1, 8)), (0, 1, 64, 4.0))
    targets = bell_draw(splits[1], (TOKENS, COLS), 1.0, 6.0, ((0, 64),))
    probe = touch_ends(jax.random.randint(splits[2], (D, COLS), 0, 2), jax.random.fold_in(splits[2], 1), 0, 1).astype(jnp.int32)
    master = bell_draw(splits[3], (D, COLS), (4 / D ** 0.5), 0.28347334, ((0, 512),), jnp.float32)
    moment = bell_draw(splits[4], (D, COLS), 0.1, 0.6, ((0, 512),), jnp.float32)
    curv = jnp.clip(jnp.exp(math.log(2.0) - 3.6888794 * jax.random.uniform(splits[5], (D, COLS), jnp.float32) ** block_levels(splits[5], (D, COLS), ((0, 512),), -0.2, 0.2)), 0.05, 2.0)
    return {"acts": acts, "targets": targets, "probe": probe, "master": master, "moment": moment, "curv": curv}


def reference(acts, targets, probe, master, moment, curv):
    weight_low = master.astype(jnp.bfloat16)
    outputs = jnp.dot(acts, weight_low, preferred_element_type=jnp.float32)
    signs = (2 * probe - 1).astype(jnp.bfloat16)
    probed = jnp.dot(acts, signs, preferred_element_type=jnp.float32)
    inverse = 1.0 / math.sqrt(TOKENS)
    slope = jnp.tanh(outputs - targets.astype(jnp.float32))
    bend = (1.0 - slope * slope) * probed
    signals = jnp.concatenate([slope * inverse, bend * inverse], axis=1).astype(jnp.bfloat16)
    terms = jnp.dot(acts.T, signals, preferred_element_type=jnp.float32)
    grad = terms[:, :COLS]
    hvp = terms[:, COLS:]
    estimate = signs.astype(jnp.float32) * hvp
    moment_out = 0.9 * moment + 0.1 * grad
    curv_out = 0.9 * curv + 0.1 * estimate
    step = jnp.clip(moment_out / jnp.maximum(0.05 * curv_out, 0.02), -1.0, 1.0)
    new_weight = (master - 0.02 * (step + 0.1 * master)).astype(jnp.bfloat16)
    return (new_weight, moment_out, curv_out)
```

```python
import math

import jax
import jax.numpy as jnp
from jax import lax
from jax.experimental import pallas as pl
from jax.experimental.pallas import tpu as pltpu
from jax.sharding import PartitionSpec as P

MESH = pl.DeviceIdType.MESH
F32 = jnp.float32
BF16 = jnp.bfloat16
NJ = 3
W = 128
A_, B_, C_, D_, E_, F_, Z_ = range(7)


def mm(a, b):
    return lax.dot_general(a, b, (((1,), (0,)), ((), ())), preferred_element_type=F32)


def mm_t(a, b):
    return lax.dot_general(a, b, (((1,), (1,)), ((), ())), preferred_element_type=F32)


def kernel(
    acts_hbm, targets_hbm, probe_hbm, master_ref, moment_ref, curv_ref,
    new_hbm, moment_out, curv_out,
    acts, probe, targets, signs, acts_pad, acts_t, sel, sel_t,
    master16, moment16, curv16, signs16,
    wbuf, nbuf, sig, obuf,
    s0, r0, s1, r1, keep0, own0, keep1, own1, tot0, tot1, probed,
    dsend, drecv, town, ysend, yrecv, ysum, zsend, zrecv,
    local_sem, rs_ss, rs_rs, ag_ss, ag_rs,
    wz_ss, wz_rs, wy_ss, wy_rs, wc_ss, wc_rs,
    d_ss, d_rs, y_ss, y_rs, z_ss, z_rs,
):
    inverse = 1.0 / math.sqrt(acts_hbm.shape[0] * lax.axis_size("dp"))
    dp = lax.axis_index("dp")
    tensor = lax.axis_index("tensor")
    y, zl, c = dp // 8, (dp // 2) % 4, dp % 2
    zh, x = tensor // 4, tensor % 4
    right, left, opp = (x + 1) % 4, (x + 3) % 4, (x + 2) % 4

    def dev(y_=None, zl_=None, c_=None, zh_=None, x_=None):
        y_ = y if y_ is None else y_
        zl_ = zl if zl_ is None else zl_
        c_ = c if c_ is None else c_
        zh_ = zh if zh_ is None else zh_
        x_ = x if x_ is None else x_
        return (y_ * 8 + zl_ * 2 + c_, zh_ * 4 + x_)

    to_right, to_left = dev(x_=right), dev(x_=left)
    to_zh, to_core = dev(zh_=1 - zh), dev(c_=1 - c)
    to_zl = [dev(zl_=(zl + i) % 4) for i in range(1, 4)]
    to_y = [dev(y_=(y + i) % 8) for i in range(1, 8)]
    own16 = pl.multiple_of(c * 512 + y * 64 + zl * 16, 16)
    own64 = pl.multiple_of(c * 512 + y * 64, 64)
    own512 = pl.multiple_of(c * 512, 512)

    def rcopy(src, dst, ss, rs, to):
        return pltpu.make_async_remote_copy(
            src_ref=src, dst_ref=dst, send_sem=ss, recv_sem=rs, device_id=to, device_id_type=MESH
        )

    sent = []

    def send(src, dst, ss, rs, to):
        copy = rcopy(src, dst, ss, rs, to)
        copy.start()
        sent.append(copy)

    def arrived(dst, rs):
        rcopy(dst, dst, rs, rs, to_core).wait_recv()

    def rows256(q):
        return pl.ds(pl.multiple_of(q * 256, 256), 256)

    loads = []
    probe_load = pltpu.make_async_copy(probe_hbm, probe, local_sem.at[0])
    probe_load.start()
    act_loads = []
    for n, q in enumerate((opp, right, left, x)):
        load = pltpu.make_async_copy(
            acts_hbm.at[rows256(q), :], acts.at[rows256(q), :], local_sem.at[1 + n]
        )
        load.start()
        act_loads.append(load)
    my_rows = pl.ds(pl.multiple_of(x * 256 + zh * 128, 128), 128)
    target_load = pltpu.make_async_copy(targets_hbm.at[my_rows, :], targets, local_sem.at[5])
    target_load.start()

    barrier = pltpu.get_barrier_semaphore()
    partners = [to_right, to_left, to_zh, to_core] + to_zl + to_y
    for to in partners:
        pl.semaphore_signal(barrier, inc=1, device_id=to, device_id_type=MESH)

    for padded, ref in ((master16, master_ref), (moment16, moment_ref), (curv16, curv_ref)):
        padded[...] = jnp.zeros_like(padded)
        padded[0:14, :] = ref[...]
    low = master16[...].astype(BF16)
    for j in range(NJ):
        wbuf[j, pl.ds(own16, 16), :] = low[:, j * W : (j + 1) * W]
    pl.semaphore_wait(barrier, len(partners))

    def gather_z(buf, k, j):
        rows = pl.ds(own16, 16)
        for i in range(3):
            send(buf.at[j, rows], buf.at[j, rows], wz_ss.at[k, j, i], wz_rs.at[k, j, i], to_zl[i])

    def gather_y(buf, k, j):
        for i in range(3):
            arrived(buf.at[j, pl.ds(0, 16)], wz_rs.at[k, j, i])
        rows = pl.ds(own64, 64)
        for i in range(7):
            send(buf.at[j, rows], buf.at[j, rows], wy_ss.at[k, j, i], wy_rs.at[k, j, i], to_y[i])

    def gather_core(buf, k, j):
        for i in range(7):
            arrived(buf.at[j, pl.ds(0, 64)], wy_rs.at[k, j, i])
        rows = pl.ds(own512, 512)
        send(buf.at[j, rows], buf.at[j, rows], wc_ss.at[k, j], wc_rs.at[k, j], to_core)

    def gathered(buf, k, j):
        arrived(buf.at[j, pl.ds(0, 512)], wc_rs.at[k, j])

    def bufs(g):
        if g == 0:
            return s0, r0, keep0, own0, tot0
        return s1.at[g - 1], r1.at[g - 1], keep1.at[g - 1], own1.at[g - 1], tot1.at[g - 1]

    def partial_sum(g, q, load):
        if g == 0:
            load.wait()
            return mm(acts[rows256(q), :], signs[...])
        return mm(acts_pad[rows256(q), :], wbuf[g - 1])

    def reduce_send(g, kind, to):
        sb, rb = bufs(g)[:2]
        send(sb.at[kind], rb.at[kind], rs_ss.at[g, kind], rs_rs.at[g, kind], to)

    def reduce_got(g, kind):
        rb = bufs(g)[1]
        arrived(rb.at[kind], rs_rs.at[g, kind])

    def reduce_1(g):
        sb, rb, keep, own, tot = bufs(g)
        part = partial_sum(g, opp, act_loads[0])
        sb[A_] = part[:128].astype(BF16)
        sb[B_] = part[128:].astype(BF16)
        reduce_send(g, A_, to_right)
        reduce_send(g, B_, to_left)
        part = partial_sum(g, right, act_loads[1])
        sb[C_] = part[128:].astype(BF16)
        reduce_send(g, C_, to_right)
        keep[0] = part[:128]
        part = partial_sum(g, left, act_loads[2])
        sb[D_] = part[:128].astype(BF16)
        reduce_send(g, D_, to_left)
        keep[1] = part[128:]
        own[...] = partial_sum(g, x, act_loads[3])

    def reduce_2(g):
        sb, rb, keep, own, tot = bufs(g)
        reduce_got(g, A_)
        sb[E_] = (keep[0] + rb[A_].astype(F32)).astype(BF16)
        reduce_send(g, E_, to_right)
        reduce_got(g, B_)
        sb[F_] = (keep[1] + rb[B_].astype(F32)).astype(BF16)
        reduce_send(g, F_, to_left)

    def reduce_3(g):
        sb, rb, keep, own, tot = bufs(g)
        for kind in (C_, D_, E_, F_):
            reduce_got(g, kind)
        tot[0] = own[0:128, :] + rb[E_].astype(F32) + rb[D_].astype(F32)
        tot[1] = own[128:256, :] + rb[C_].astype(F32) + rb[F_].astype(F32)
        sb[Z_] = tot[1 - zh].astype(BF16)
        reduce_send(g, Z_, to_zh)

    def reduce_4(g):
        sb, rb, keep, own, tot = bufs(g)
        reduce_got(g, Z_)
        return tot[zh] + rb[Z_].astype(F32)

    def piece(q, h):
        return pl.ds(pl.multiple_of(q * 256 + h * 128, 128), 128)

    def signal_send(j, q, h, idx, to):
        rows = piece(q, h)
        send(sig.at[j, rows], sig.at[j, rows], ag_ss.at[j, idx], ag_rs.at[j, idx], to)

    def signal_got(j, idx):
        arrived(sig.at[j, pl.ds(0, 128)], ag_rs.at[j, idx])

    def signal_a(j):
        out = reduce_4(1 + j)
        cols = slice(j * W, (j + 1) * W)
        slope = jnp.tanh(out - targets[:, cols].astype(F32))
        bend = (1.0 - slope * slope) * probed[:, cols]
        rows = piece(x, zh)
        sig[j, rows, 0:W] = (slope * inverse).astype(BF16)
        sig[j, rows, W : 2 * W] = (bend * inverse).astype(BF16)
        signal_send(j, x, zh, 0, to_zh)
        signal_send(j, x, zh, 1 + zh, to_right)
        signal_send(j, x, zh, 3 + zh, to_left)

    def signal_b(j):
        signal_got(j, 0)
        signal_send(j, x, 1 - zh, 2 - zh, to_right)
        signal_send(j, x, 1 - zh, 4 - zh, to_left)

    def signal_c(j):
        signal_got(j, 1)
        signal_send(j, left, 0, 5, to_right)
        signal_got(j, 4)
        signal_send(j, right, 1, 6, to_left)

    def signal_d(j):
        for idx in (2, 3, 5, 6):
            signal_got(j, idx)

    def terms_core(j):
        other = pl.ds(pl.multiple_of((1 - c) * 512, 512), 512)
        mine = pl.ds(own512, 512)
        dsend[j] = mm(acts_t[other, :], sig[j]).astype(BF16)
        send(dsend.at[j], drecv.at[j], d_ss.at[j], d_rs.at[j], to_core)
        town[j] = mm(acts_t[mine, :], sig[j])

    def terms_y(j):
        arrived(drecv.at[j], d_rs.at[j])
        town[j] = town[j] + drecv[j].astype(F32)
        ysend[j] = town[j].astype(BF16)
        for i in range(7):
            rows = pl.ds(pl.multiple_of(((y + 1 + i) % 8) * 64, 64), 64)
            send(ysend.at[j, rows], yrecv.at[j, i], y_ss.at[j, i], y_rs.at[j, i], to_y[i])

    def terms_z(j):
        for i in range(7):
            arrived(yrecv.at[j, i], y_rs.at[j, i])
        total = town[j, pl.ds(pl.multiple_of(y * 64, 64), 64), :]
        for i in range(7):
            total = total + yrecv[j, i].astype(F32)
        ysum[j] = total
        zsend[j] = total.astype(BF16)
        for i in range(3):
            rows = pl.ds(pl.multiple_of(((zl + 1 + i) % 4) * 16, 16), 16)
            send(zsend.at[j, rows], zrecv.at[j, i], z_ss.at[j, i], z_rs.at[j, i], to_zl[i])

    def update(j):
        for i in range(3):
            arrived(zrecv.at[j, i], z_rs.at[j, i])
        total = ysum[j, pl.ds(pl.multiple_of(zl * 16, 16), 16), :]
        for i in range(3):
            total = total + zrecv[j, i].astype(F32)
        grad, hvp = total[:, :W], total[:, W:]
        cols = slice(j * W, (j + 1) * W)
        estimate = signs16[:, cols] * hvp
        moment = 0.9 * moment16[:, cols] + 0.1 * grad
        curv = 0.9 * curv16[:, cols] + 0.1 * estimate
        moment_out[:, cols] = moment[0:14]
        curv_out[:, cols] = curv[0:14]
        step = jnp.clip(moment / jnp.maximum(0.05 * curv, 0.02), -1.0, 1.0)
        master = master16[:, cols]
        updated = master - 0.02 * (step + 0.1 * master)
        real = lax.broadcasted_iota(jnp.int32, updated.shape, 0) < 14
        nbuf[j, pl.ds(own16, 16), :] = jnp.where(real, updated, 0.0).astype(BF16)
        gather_z(nbuf, 1, j)

    stores = []

    def finish(j):
        gathered(nbuf, 1, j)
        obuf[j] = mm(sel_t[...], nbuf[j]).astype(BF16)
        store = pltpu.make_async_copy(
            obuf.at[j], new_hbm.at[:, pl.ds(j * W, W)], local_sem.at[6 + j]
        )
        store.start()
        stores.append(store)

    for j in range(NJ):
        gather_z(wbuf, 0, j)
    probe_load.wait()
    signs[...] = (2 * probe[...] - 1).astype(F32).astype(BF16)
    reduce_1(0)
    for j in range(NJ):
        gather_y(wbuf, 0, j)
    reduce_2(0)

    def source(p):
        r = p % 16
        row = (((p // 64) % 8) * 8 + ((p // 16) % 4) * 2 + p // 512) * 14 + r
        return jnp.where(r < 14, row, -1)

    @pl.loop(0, 7)
    def _(t):
        rows = pl.ds(pl.multiple_of(t * 128, 128), 128)
        k = lax.broadcasted_iota(jnp.int32, (128, 1024), 0) + t * 128
        p = source(lax.broadcasted_iota(jnp.int32, (1, 1024), 1))
        sel_t[rows, :] = jnp.where(k == p, 1.0, 0.0).astype(BF16)

    @pl.loop(0, 4)
    def _(t):
        rows = pl.ds(pl.multiple_of(t * 256, 256), 256)
        acts_pad[rows, :] = mm(acts[rows, :], sel_t[...]).astype(BF16)

    reduce_3(0)
    gather_core(wbuf, 0, 0)
    gathered(wbuf, 0, 0)
    reduce_1(1)
    gather_core(wbuf, 0, 1)
    reduce_2(1)
    gathered(wbuf, 0, 1)
    reduce_1(2)
    gather_core(wbuf, 0, 2)
    probed[...] = reduce_4(0)
    reduce_3(1)
    reduce_2(2)
    gathered(wbuf, 0, 2)
    reduce_1(3)

    @pl.loop(0, 8)
    def _(t):
        rows = pl.ds(pl.multiple_of(t * 128, 128), 128)
        k = lax.broadcasted_iota(jnp.int32, (128, 896), 1)
        p = source(lax.broadcasted_iota(jnp.int32, (128, 1), 0) + t * 128)
        sel[rows, :] = jnp.where(k == p, 1.0, 0.0).astype(BF16)

    target_load.wait()
    reduce_3(2)
    signal_a(0)
    reduce_2(3)

    @pl.loop(0, 4)
    def _(t):
        rows = pl.ds(pl.multiple_of(t * 256, 256), 256)
        acts_t[rows, :] = mm_t(sel[rows, :], acts[...]).astype(BF16)

    signs16[...] = mm(sel[pl.ds(own16, 16), :], signs[...])
    reduce_3(3)
    signal_b(0)
    signal_a(1)
    signal_c(0)
    signal_a(2)
    signal_b(1)
    signal_d(0)
    terms_core(0)
    signal_c(1)
    signal_b(2)
    terms_y(0)
    signal_d(1)
    terms_core(1)
    signal_c(2)
    terms_z(0)
    terms_y(1)
    update(0)
    signal_d(2)
    terms_core(2)
    terms_z(1)
    gather_y(nbuf, 1, 0)
    terms_y(2)
    update(1)
    gather_core(nbuf, 1, 0)
    terms_z(2)
    gather_y(nbuf, 1, 1)
    finish(0)
    update(2)
    gather_core(nbuf, 1, 1)
    gather_y(nbuf, 1, 2)
    finish(1)
    gather_core(nbuf, 1, 2)
    finish(2)
    for store in stores:
        store.wait()
    for copy in sent:
        copy.wait_send()


def body(acts, targets, probe, master, moment, curv):
    any_spec = pl.BlockSpec(memory_space=pl.ANY)
    vmem_spec = pl.BlockSpec(memory_space=pltpu.VMEM)
    dma = pltpu.SemaphoreType.DMA
    vm = pltpu.VMEM
    return pl.pallas_call(
        kernel,
        out_shape=(
            jax.ShapeDtypeStruct((896, 384), BF16),
            jax.ShapeDtypeStruct((14, 384), F32),
            jax.ShapeDtypeStruct((14, 384), F32),
        ),
        in_specs=[any_spec, any_spec, any_spec, vmem_spec, vmem_spec, vmem_spec],
        out_specs=(any_spec, vmem_spec, vmem_spec),
        scratch_shapes=[
            vm((1024, 896), BF16), vm((896, 384), jnp.int32), vm((128, 384), BF16),
            vm((896, 384), BF16), vm((1024, 1024), BF16), vm((1024, 1024), BF16),
            vm((1024, 896), BF16), vm((896, 1024), BF16),
            vm((16, 384), F32), vm((16, 384), F32), vm((16, 384), F32), vm((16, 384), F32),
            vm((NJ, 1024, W), BF16), vm((NJ, 1024, W), BF16),
            vm((NJ, 1024, 2 * W), BF16), vm((NJ, 896, W), BF16),
            vm((7, 128, 384), BF16), vm((7, 128, 384), BF16),
            vm((NJ, 7, 128, W), BF16), vm((NJ, 7, 128, W), BF16),
            vm((2, 128, 384), F32), vm((256, 384), F32),
            vm((NJ, 2, 128, W), F32), vm((NJ, 256, W), F32),
            vm((2, 128, 384), F32), vm((NJ, 2, 128, W), F32), vm((128, 384), F32),
            vm((NJ, 512, 2 * W), BF16), vm((NJ, 512, 2 * W), BF16), vm((NJ, 512, 2 * W), F32),
            vm((NJ, 512, 2 * W), BF16), vm((NJ, 7, 64, 2 * W), BF16), vm((NJ, 64, 2 * W), F32),
            vm((NJ, 64, 2 * W), BF16), vm((NJ, 3, 16, 2 * W), BF16),
            dma((9,)), dma((4, 7)), dma((4, 7)), dma((NJ, 7)), dma((NJ, 7)),
            dma((2, NJ, 3)), dma((2, NJ, 3)), dma((2, NJ, 7)), dma((2, NJ, 7)),
            dma((2, NJ)), dma((2, NJ)),
            dma((NJ,)), dma((NJ,)), dma((NJ, 7)), dma((NJ, 7)), dma((NJ, 3)), dma((NJ, 3)),
        ],
        compiler_params=pltpu.CompilerParams(
            collective_id=0, has_side_effects=True, vmem_limit_bytes=56 * 2**20
        ),
        name="sophia",
    )(acts, targets, probe, master, moment, curv)


def solution(mesh):
    in_specs = (
        P("dp", "tensor"),
        P("dp", None),
        P("tensor", None),
        P(("tensor", "dp"), None),
        P(("tensor", "dp"), None),
        P(("tensor", "dp"), None),
    )
    out_specs = (P("tensor", None), P(("tensor", "dp"), None), P(("tensor", "dp"), None))
    return jax.shard_map(body, mesh=mesh, in_specs=in_specs, out_specs=out_specs, check_vma=False)
```

```python
import math

import jax
import jax.numpy as jnp
from jax import lax
from jax.experimental import pallas as pl
from jax.experimental.pallas import tpu as pltpu
from jax.sharding import PartitionSpec as P

MESH = pl.DeviceIdType.MESH
F32 = jnp.float32
BF16 = jnp.bfloat16
NJ = 3
W = 128
A_, B_, C_, D_, E_, F_, Z_ = range(7)


def mm(a, b):
    return lax.dot_general(a, b, (((1,), (0,)), ((), ())), preferred_element_type=F32)


def mm_t(a, b):
    return lax.dot_general(a, b, (((1,), (1,)), ((), ())), preferred_element_type=F32)


def kernel(
    acts_hbm, targets_hbm, probe_hbm, master_ref, moment_ref, curv_ref,
    new_hbm, moment_out, curv_out,
    acts, probe, targets, signs, acts_pad, sel_t,
    master16, moment16, curv16, signs16,
    wbuf, nbuf, sig, obuf,
    s0, r0, s1, r1, keep0, own0, keep1, own1, tot0, tot1, probed,
    dsend, drecv, town, tsend, recv_a1, recv_b1, sum_a, sum_b, send_a2, send_b2, recv_a2, recv_b2,
    local_sem, rs_ss, rs_rs, ag_ss, ag_rs,
    wa_ss, wa_rs, wc_ss, wc_rs, d_ss, d_rs, t_ss, t_rs,
):
    inverse = 1.0 / math.sqrt(acts_hbm.shape[0] * lax.axis_size("dp"))
    dp = lax.axis_index("dp")
    tensor = lax.axis_index("tensor")
    y, zl, c = dp // 8, (dp // 2) % 4, dp % 2
    zh, x = tensor // 4, tensor % 4
    right, left, opp = (x + 1) % 4, (x + 3) % 4, (x + 2) % 4

    def dev(y_=None, zl_=None, c_=None, zh_=None, x_=None):
        y_ = y if y_ is None else y_
        zl_ = zl if zl_ is None else zl_
        c_ = c if c_ is None else c_
        zh_ = zh if zh_ is None else zh_
        x_ = x if x_ is None else x_
        return (y_ * 8 + zl_ * 2 + c_, zh_ * 4 + x_)

    to_right, to_left = dev(x_=right), dev(x_=left)
    to_zh, to_core = dev(zh_=1 - zh), dev(c_=1 - c)
    to_zl = [dev(zl_=(zl + i) % 4) for i in range(1, 4)]
    to_y = [dev(y_=(y + i) % 8) for i in range(1, 8)]

    def ring(i):
        return (y + 4 + i // 4) % 8, (zl + 2 + i % 4) % 4

    def each_peer(send_to):
        def visit(i, _):
            i = i + jnp.where(i >= 18, 1, 0)
            send_to(i, *ring(i))
            return 0

        lax.fori_loop(0, 31, visit, 0)

    own16 = pl.multiple_of(c * 512 + y * 64 + zl * 16, 16)
    own512 = pl.multiple_of(c * 512, 512)

    def rcopy(src, dst, ss, rs, to):
        return pltpu.make_async_remote_copy(
            src_ref=src, dst_ref=dst, send_sem=ss, recv_sem=rs, device_id=to, device_id_type=MESH
        )

    sent, bulk = [], []

    def send(src, dst, sems, to):
        ss, rs, at = sems
        copy = rcopy(src, dst, ss.at[at], rs.at[at], to)
        copy.start()
        sent.append(copy)

    def arrived(dst, rs, at):
        rcopy(dst, dst, rs.at[at], rs.at[at], to_core).wait_recv()

    def rows256(q):
        return pl.ds(pl.multiple_of(q * 256, 256), 256)

    loads = []
    probe_load = pltpu.make_async_copy(probe_hbm, probe, local_sem.at[0])
    probe_load.start()
    act_loads = []
    for n, q in enumerate((opp, right, left, x)):
        load = pltpu.make_async_copy(
            acts_hbm.at[rows256(q), :], acts.at[rows256(q), :], local_sem.at[1 + n]
        )
        load.start()
        act_loads.append(load)
    my_rows = pl.ds(pl.multiple_of(x * 256 + zh * 128, 128), 128)
    target_load = pltpu.make_async_copy(targets_hbm.at[my_rows, :], targets, local_sem.at[5])
    target_load.start()

    barrier = pltpu.get_barrier_semaphore()
    near = [to_right, to_left, to_zh, to_core]
    for to in near:
        pl.semaphore_signal(barrier, inc=1, device_id=to, device_id_type=MESH)

    def greet(i, y_, zl_):
        pl.semaphore_signal(barrier, inc=1, device_id=dev(y_=y_, zl_=zl_), device_id_type=MESH)

    each_peer(greet)

    def meet():
        pl.semaphore_wait(barrier, len(near) + 31)

    def load_rows():
        for padded, ref in ((master16, master_ref), (moment16, moment_ref), (curv16, curv_ref)):
            padded[...] = jnp.zeros_like(padded)
            padded[0:14, :] = ref[...]
        low = master16[...].astype(BF16)
        for j in range(NJ):
            wbuf[j, pl.ds(own16, 16), :] = low[:, j * W : (j + 1) * W]

    def gather_all(buf, k, j, count=1):
        rows = pl.ds(own16, 16)
        js = pl.ds(j, count)

        def visit(i, y_, zl_):
            rcopy(
                buf.at[js, rows], buf.at[js, rows], wa_ss.at[k, j], wa_rs.at[k, j],
                dev(y_=y_, zl_=zl_),
            ).start()

        each_peer(visit)
        bulk.append((buf.at[js, pl.ds(0, 496)], wa_ss, (k, j)))

    def gather_core(buf, k, j, count=1):
        js = pl.ds(j, count)
        arrived(buf.at[js, pl.ds(0, 496)], wa_rs, (k, j))
        rows = pl.ds(own512, 512)
        send(buf.at[js, rows], buf.at[js, rows], (wc_ss, wc_rs, (k, j)), to_core)

    def gathered(buf, k, j, count=1):
        arrived(buf.at[pl.ds(j, count), pl.ds(0, 512)], wc_rs, (k, j))

    def bufs(g):
        if g == 0:
            return s0, r0, keep0, own0, tot0
        return s1.at[g - 1], r1.at[g - 1], keep1.at[g - 1], own1.at[g - 1], tot1.at[g - 1]

    def partial_sum(g, q, load):
        if g == 0:
            load.wait()
            return mm(acts[rows256(q), :], signs[...])
        return mm(acts_pad[rows256(q), :], wbuf[g - 1])

    def reduce_send(g, kind, to):
        sb, rb = bufs(g)[:2]
        send(sb.at[kind], rb.at[kind], (rs_ss, rs_rs, (g, kind,)), to)

    def reduce_got(g, kind):
        rb = bufs(g)[1]
        arrived(rb.at[kind], rs_rs, (g, kind,))

    def reduce_0(g):
        sb = bufs(g)[0]
        part = partial_sum(g, opp, act_loads[0])
        sb[A_] = part[:128].astype(BF16)
        sb[B_] = part[128:].astype(BF16)

    def reduce_1(g):
        sb, rb, keep, own, tot = bufs(g)
        reduce_send(g, A_, to_right)
        reduce_send(g, B_, to_left)
        part = partial_sum(g, right, act_loads[1])
        sb[C_] = part[128:].astype(BF16)
        reduce_send(g, C_, to_right)
        keep[0] = part[:128]
        part = partial_sum(g, left, act_loads[2])
        sb[D_] = part[:128].astype(BF16)
        reduce_send(g, D_, to_left)
        keep[1] = part[128:]
        own[...] = partial_sum(g, x, act_loads[3])

    def reduce_2(g):
        sb, rb, keep, own, tot = bufs(g)
        reduce_got(g, A_)
        sb[E_] = (keep[0] + rb[A_].astype(F32)).astype(BF16)
        reduce_send(g, E_, to_right)
        reduce_got(g, B_)
        sb[F_] = (keep[1] + rb[B_].astype(F32)).astype(BF16)
        reduce_send(g, F_, to_left)

    def reduce_3(g):
        sb, rb, keep, own, tot = bufs(g)
        for kind in (C_, D_, E_, F_):
            reduce_got(g, kind)
        tot[0] = own[0:128, :] + rb[E_].astype(F32) + rb[D_].astype(F32)
        tot[1] = own[128:256, :] + rb[C_].astype(F32) + rb[F_].astype(F32)
        sb[Z_] = tot[1 - zh].astype(BF16)
        reduce_send(g, Z_, to_zh)

    def reduce_4(g):
        sb, rb, keep, own, tot = bufs(g)
        reduce_got(g, Z_)
        return tot[zh] + rb[Z_].astype(F32)

    def piece(q, h):
        return pl.ds(pl.multiple_of(q * 256 + h * 128, 128), 128)

    def signal_send(j, q, h, idx, to):
        rows = piece(q, h)
        send(sig.at[j, rows], sig.at[j, rows], (ag_ss, ag_rs, (j, idx,)), to)

    def signal_got(j, idx):
        arrived(sig.at[j, pl.ds(0, 128)], ag_rs, (j, idx,))

    def signal_a(j):
        out = reduce_4(1 + j)
        cols = slice(j * W, (j + 1) * W)
        slope = jnp.tanh(out - targets[:, cols].astype(F32))
        bend = (1.0 - slope * slope) * probed[:, cols]
        rows = piece(x, zh)
        sig[j, rows, 0:W] = (slope * inverse).astype(BF16)
        sig[j, rows, W : 2 * W] = (bend * inverse).astype(BF16)
        signal_send(j, x, zh, 0, to_zh)
        signal_send(j, x, zh, 1 + zh, to_right)
        signal_send(j, x, zh, 3 + zh, to_left)

    def signal_b(j):
        signal_got(j, 0)
        signal_send(j, x, 1 - zh, 2 - zh, to_right)
        signal_send(j, x, 1 - zh, 4 - zh, to_left)

    def signal_c(j):
        signal_got(j, 1)
        signal_send(j, left, 0, 5, to_right)
        signal_got(j, 4)
        signal_send(j, right, 1, 6, to_left)

    def signal_d(j):
        for idx in (2, 3, 5, 6):
            signal_got(j, idx)

    def contract(rows, j):
        return lax.dot_general(
            acts_pad[:, rows], sig[j], (((0,), (0,)), ((), ())), preferred_element_type=F32
        )

    def terms_core(j):
        dsend[j] = contract(pl.ds(pl.multiple_of((1 - c) * 512, 512), 512), j).astype(BF16)
        send(dsend.at[j], drecv.at[j], (d_ss, d_rs, (j,)), to_core)
        town[j] = contract(pl.ds(own512, 512), j).reshape(8, 4, 16, 2 * W)

    def bulk_send(j, phase, pairs, whole):
        for src, dst, to in pairs:
            rcopy(src, dst, t_ss.at[j, phase], t_rs.at[j, phase], to).start()
        bulk.append((whole, t_ss, (j, phase)))

    def terms_1(j):
        arrived(drecv.at[j], d_rs, (j,))
        total = town[j] + drecv[j].astype(F32).reshape(8, 4, 16, 2 * W)
        town[j] = total
        tsend[j, 0] = total[..., :W].astype(BF16)
        tsend[j, 1] = total[..., W:].astype(BF16)
        bulk_send(
            j, 1,
            [(tsend.at[j, 1, :, (zl + 1 + i) % 4], recv_b1.at[j, i], to_zl[i]) for i in range(3)],
            recv_b1.at[j],
        )
        bulk_send(
            j, 0,
            [(tsend.at[j, 0, (y + 1 + i) % 8], recv_a1.at[j, i], to_y[i]) for i in range(7)],
            recv_a1.at[j],
        )

    def terms_2(j):
        arrived(recv_a1.at[j], t_rs, (j, 0))
        total = town[j, y, :, :, 0:W]
        for i in range(7):
            total = total + recv_a1[j, i].astype(F32)
        sum_a[j] = total
        send_a2[j] = total.astype(BF16)
        bulk_send(
            j, 2,
            [(send_a2.at[j, (zl + 1 + i) % 4], recv_a2.at[j, i], to_zl[i]) for i in range(3)],
            recv_a2.at[j],
        )
        arrived(recv_b1.at[j], t_rs, (j, 1))
        total = town[j, :, zl, :, W : 2 * W]
        for i in range(3):
            total = total + recv_b1[j, i].astype(F32)
        sum_b[j] = total
        send_b2[j] = total.astype(BF16)
        bulk_send(
            j, 3,
            [(send_b2.at[j, (y + 1 + i) % 8], recv_b2.at[j, i], to_y[i]) for i in range(7)],
            recv_b2.at[j],
        )

    def update(j):
        arrived(recv_a2.at[j], t_rs, (j, 2))
        grad = sum_a[j, zl]
        for i in range(3):
            grad = grad + recv_a2[j, i].astype(F32)
        arrived(recv_b2.at[j], t_rs, (j, 3))
        hvp = sum_b[j, y]
        for i in range(7):
            hvp = hvp + recv_b2[j, i].astype(F32)
        cols = slice(j * W, (j + 1) * W)
        estimate = signs16[:, cols] * hvp
        moment = 0.9 * moment16[:, cols] + 0.1 * grad
        curv = 0.9 * curv16[:, cols] + 0.1 * estimate
        moment_out[:, cols] = moment[0:14]
        curv_out[:, cols] = curv[0:14]
        step = jnp.clip(moment / jnp.maximum(0.05 * curv, 0.02), -1.0, 1.0)
        master = master16[:, cols]
        updated = master - 0.02 * (step + 0.1 * master)
        real = lax.broadcasted_iota(jnp.int32, updated.shape, 0) < 14
        nbuf[j, pl.ds(own16, 16), :] = jnp.where(real, updated, 0.0).astype(BF16)
        gather_all(nbuf, 1, j)

    stores = []

    def finish(j):
        gathered(nbuf, 1, j)
        obuf[j] = mm(sel_t[...], nbuf[j]).astype(BF16)
        store = pltpu.make_async_copy(
            obuf.at[j], new_hbm.at[:, pl.ds(j * W, W)], local_sem.at[6 + j]
        )
        store.start()
        stores.append(store)

    def source(p):
        r = p % 16
        row = (((p // 64) % 8) * 8 + ((p // 16) % 4) * 2 + p // 512) * 14 + r
        return jnp.where(r < 14, row, -1)

    def make_signs():
        probe_load.wait()
        signs[...] = (2 * probe[...] - 1).astype(F32).astype(BF16)

    def make_sel_t():
        @pl.loop(0, 7)
        def _(t):
            rows = pl.ds(pl.multiple_of(t * 128, 128), 128)
            k = lax.broadcasted_iota(jnp.int32, (128, 1024), 0) + t * 128
            p = source(lax.broadcasted_iota(jnp.int32, (1, 1024), 1))
            sel_t[rows, :] = jnp.where(k == p, 1.0, 0.0).astype(BF16)

    def make_acts_pad(first, last):
        @pl.loop(first, last)
        def _(t):
            rows = pl.ds(pl.multiple_of(t * 256, 256), 256)
            acts_pad[rows, :] = mm(acts[rows, :], sel_t[...]).astype(BF16)

    def make_signs16():
        p = source(lax.broadcasted_iota(jnp.int32, (16, 1), 0) + own16)
        k = lax.broadcasted_iota(jnp.int32, (16, 896), 1)
        signs16[...] = mm(jnp.where(k == p, 1.0, 0.0).astype(BF16), signs[...])

    def keep_probed():
        probed[...] = reduce_4(0)

    steps = [
        (load_rows,), (make_signs,), (reduce_0, 0), (meet,),
        (gather_all, wbuf, 0, 0), (reduce_1, 0), (gather_all, wbuf, 0, 1),
        (gather_all, wbuf, 0, 2),
        (make_sel_t,), (make_acts_pad, 0, 2), (reduce_2, 0), (make_acts_pad, 2, 4),
        (make_signs16,), (gather_core, wbuf, 0, 0), (reduce_3, 0), (gathered, wbuf, 0, 0),
        (reduce_0, 1), (reduce_1, 1), (gather_core, wbuf, 0, 1), (reduce_2, 1),
        (gathered, wbuf, 0, 1), (reduce_0, 2), (reduce_1, 2), (gather_core, wbuf, 0, 2),
        (keep_probed,), (reduce_3, 1), (gathered, wbuf, 0, 2), (reduce_0, 3), (reduce_1, 3),
        (reduce_2, 2), (target_load.wait,), (reduce_2, 3), (reduce_3, 2), (signal_a, 0),
        (reduce_3, 3), (signal_b, 0), (signal_a, 1), (signal_c, 0), (signal_a, 2),
        (signal_b, 1), (signal_b, 2), (signal_c, 1), (signal_d, 0), (terms_core, 0),
        (signal_c, 2), (terms_1, 0), (signal_d, 1), (terms_core, 1), (terms_1, 1),
        (signal_d, 2), (terms_core, 2), (terms_2, 0), (terms_1, 2), (terms_2, 1), (update, 0),
        (terms_2, 2), (update, 1), (update, 2), (gather_core, nbuf, 1, 0),
        (gather_core, nbuf, 1, 1), (finish, 0), (finish, 1), (gather_core, nbuf, 1, 2),
        (finish, 2),
    ]
    for step, *values in steps:
        step(*values)
    for store in stores:
        store.wait()
    for copy in sent:
        copy.wait_send()
    for ref, ss, at in bulk:
        rcopy(ref, ref, ss.at[at], ss.at[at], to_core).wait_send()


def copy_kernel(*refs):
    count = len(refs) // 2
    for n in range(count):
        refs[count + n][...] = refs[n][...]


def body(acts, targets, probe, master, moment, curv):
    any_spec = pl.BlockSpec(memory_space=pl.ANY)
    vmem_spec = pl.BlockSpec(memory_space=pltpu.VMEM)
    dma = pltpu.SemaphoreType.DMA
    vm = pltpu.VMEM
    shapes = (
        jax.ShapeDtypeStruct((896, 384), BF16),
        jax.ShapeDtypeStruct((14, 384), F32),
        jax.ShapeDtypeStruct((14, 384), F32),
    )
    results = pl.pallas_call(
        kernel,
        out_shape=shapes,
        in_specs=[any_spec, any_spec, any_spec, vmem_spec, vmem_spec, vmem_spec],
        out_specs=(any_spec, vmem_spec, vmem_spec),
        scratch_shapes=[
            vm((1024, 896), BF16), vm((896, 384), jnp.int32), vm((128, 384), BF16),
            vm((896, 384), BF16), vm((1024, 1024), BF16), vm((896, 1024), BF16),
            vm((16, 384), F32), vm((16, 384), F32), vm((16, 384), F32), vm((16, 384), F32),
            vm((NJ, 1024, W), BF16), vm((NJ, 1024, W), BF16),
            vm((NJ, 1024, 2 * W), BF16), vm((NJ, 896, W), BF16),
            vm((7, 128, 384), BF16), vm((7, 128, 384), BF16),
            vm((NJ, 7, 128, W), BF16), vm((NJ, 7, 128, W), BF16),
            vm((2, 128, 384), F32), vm((256, 384), F32),
            vm((NJ, 2, 128, W), F32), vm((NJ, 256, W), F32),
            vm((2, 128, 384), F32), vm((NJ, 2, 128, W), F32), vm((128, 384), F32),
            vm((NJ, 512, 2 * W), BF16), vm((NJ, 512, 2 * W), BF16), vm((NJ, 8, 4, 16, 2 * W), F32),
            vm((NJ, 2, 8, 4, 16, W), BF16), vm((NJ, 7, 4, 16, W), BF16), vm((NJ, 3, 8, 16, W), BF16),
            vm((NJ, 4, 16, W), F32), vm((NJ, 8, 16, W), F32),
            vm((NJ, 4, 16, W), BF16), vm((NJ, 8, 16, W), BF16),
            vm((NJ, 3, 16, W), BF16), vm((NJ, 7, 16, W), BF16),
            dma((9,)), dma((4, 7)), dma((4, 7)), dma((NJ, 7)), dma((NJ, 7)),
            dma((2, NJ)), dma((2, NJ)), dma((2, NJ)), dma((2, NJ)),
            dma((NJ,)), dma((NJ,)), dma((NJ, 4)), dma((NJ, 4)),
        ],
        compiler_params=pltpu.CompilerParams(
            collective_id=0, has_side_effects=True, vmem_limit_bytes=56 * 2**20
        ),
        name="sophia",
    )(acts, targets, probe, master, moment, curv)
    return pl.pallas_call(
        copy_kernel,
        out_shape=shapes,
        in_specs=[vmem_spec] * 3,
        out_specs=(vmem_spec,) * 3,
        name="write_out",
    )(*results)


def solution(mesh):
    in_specs = (
        P("dp", "tensor"),
        P("dp", None),
        P("tensor", None),
        P(("tensor", "dp"), None),
        P(("tensor", "dp"), None),
        P(("tensor", "dp"), None),
    )
    out_specs = (P("tensor", None), P(("tensor", "dp"), None), P(("tensor", "dp"), None))
    return jax.shard_map(body, mesh=mesh, in_specs=in_specs, out_specs=out_specs, check_vma=False)
```

```python
import math

import jax
import jax.numpy as jnp
from jax import lax
from jax.experimental import pallas as pl
from jax.experimental.pallas import tpu as pltpu
from jax.sharding import PartitionSpec as P

MESH = pl.DeviceIdType.MESH
F32 = jnp.float32
BF16 = jnp.bfloat16
NJ = 3
W = 128
A_, B_, C_, D_, E_, F_ = range(6)


def mm(a, b):
    return lax.dot_general(a, b, (((1,), (0,)), ((), ())), preferred_element_type=F32)


def mm_t(a, b):
    return lax.dot_general(a, b, (((1,), (1,)), ((), ())), preferred_element_type=F32)


def kernel(
    acts_hbm, targets_hbm, probe_hbm, master_ref, moment_ref, curv_ref,
    new_hbm, moment_out, curv_out,
    acts, probe, targets, signs, acts_pad, sel_t,
    master16, moment16, curv16, signs16,
    wbuf, nbuf, sig, obuf,
    s0, r0, s1, r1, keep0, own0, keep1, own1, tot0, tot1, swap_out, swap_in,
    dsend, drecv, town, tsend, recv_a1, recv_b1, sum_a, sum_b, send_a2, send_b2, recv_a2, recv_b2,
    local_sem, rs_ss, rs_rs, sw_ss, sw_rs, ag_ss, ag_rs,
    wa_ss, wa_rs, wc_ss, wc_rs, d_ss, d_rs, t_ss, t_rs,
):
    inverse = 1.0 / math.sqrt(acts_hbm.shape[0] * lax.axis_size("dp"))
    dp = lax.axis_index("dp")
    tensor = lax.axis_index("tensor")
    y, zl, c = dp // 8, (dp // 2) % 4, dp % 2
    zh, x = tensor // 4, tensor % 4
    right, left, opp = (x + 1) % 4, (x + 3) % 4, (x + 2) % 4

    def dev(y_=None, zl_=None, c_=None, zh_=None, x_=None):
        y_ = y if y_ is None else y_
        zl_ = zl if zl_ is None else zl_
        c_ = c if c_ is None else c_
        zh_ = zh if zh_ is None else zh_
        x_ = x if x_ is None else x_
        return (y_ * 8 + zl_ * 2 + c_, zh_ * 4 + x_)

    to_right, to_left = dev(x_=right), dev(x_=left)
    to_zh, to_core = dev(zh_=1 - zh), dev(c_=1 - c)
    to_zl = [dev(zl_=(zl + i) % 4) for i in range(1, 4)]
    to_y = [dev(y_=(y + i) % 8) for i in range(1, 8)]

    def ring(i):
        return (y + 4 + i // 4) % 8, (zl + 2 + i % 4) % 4

    def each_peer(send_to):
        def visit(i, _):
            i = i + jnp.where(i >= 18, 1, 0)
            send_to(i, *ring(i))
            return 0

        lax.fori_loop(0, 31, visit, 0)

    own16 = pl.multiple_of(c * 512 + y * 64 + zl * 16, 16)
    own512 = pl.multiple_of(c * 512, 512)

    def rcopy(src, dst, ss, rs, to):
        return pltpu.make_async_remote_copy(
            src_ref=src, dst_ref=dst, send_sem=ss, recv_sem=rs, device_id=to, device_id_type=MESH
        )

    sent, bulk = [], []

    def send(src, dst, sems, to):
        ss, rs, at = sems
        copy = rcopy(src, dst, ss.at[at], rs.at[at], to)
        copy.start()
        sent.append(copy)

    def arrived(dst, rs, at):
        rcopy(dst, dst, rs.at[at], rs.at[at], to_core).wait_recv()

    def rows256(q):
        return pl.ds(pl.multiple_of(q * 256, 256), 256)

    loads = []
    probe_load = pltpu.make_async_copy(probe_hbm, probe, local_sem.at[0])
    probe_load.start()
    act_loads = []
    for n, q in enumerate((opp, right, left, x)):
        load = pltpu.make_async_copy(
            acts_hbm.at[rows256(q), :], acts.at[rows256(q), :], local_sem.at[1 + n]
        )
        load.start()
        act_loads.append(load)
    target_load = pltpu.make_async_copy(targets_hbm.at[rows256(x), :], targets, local_sem.at[5])
    target_load.start()

    barrier = pltpu.get_barrier_semaphore()
    near = [to_right, to_left, to_zh, to_core]
    for to in near:
        pl.semaphore_signal(barrier, inc=1, device_id=to, device_id_type=MESH)

    def greet(i, y_, zl_):
        pl.semaphore_signal(barrier, inc=1, device_id=dev(y_=y_, zl_=zl_), device_id_type=MESH)

    each_peer(greet)

    def meet():
        pl.semaphore_wait(barrier, len(near) + 31)

    def load_rows():
        for padded, ref in ((master16, master_ref), (moment16, moment_ref), (curv16, curv_ref)):
            padded[...] = jnp.zeros_like(padded)
            padded[0:14, :] = ref[...]
        low = master16[...].astype(BF16)
        for j in range(NJ):
            wbuf[j, pl.ds(own16, 16), :] = low[:, j * W : (j + 1) * W]

    def gather_all(buf, k, j, count=1):
        rows = pl.ds(own16, 16)
        js = pl.ds(j, count)

        def visit(i, y_, zl_):
            rcopy(
                buf.at[js, rows], buf.at[js, rows], wa_ss.at[k, j], wa_rs.at[k, j],
                dev(y_=y_, zl_=zl_),
            ).start()

        each_peer(visit)
        bulk.append((buf.at[js, pl.ds(0, 496)], wa_ss, (k, j)))

    def gather_core(buf, k, j, count=1):
        js = pl.ds(j, count)
        arrived(buf.at[js, pl.ds(0, 496)], wa_rs, (k, j))
        rows = pl.ds(own512, 512)
        send(buf.at[js, rows], buf.at[js, rows], (wc_ss, wc_rs, (k, j)), to_core)

    def gathered(buf, k, j, count=1):
        arrived(buf.at[pl.ds(j, count), pl.ds(0, 512)], wc_rs, (k, j))

    def bufs(g):
        if g == 0:
            return s0, r0, keep0, own0, tot0
        return s1.at[g - 1], r1.at[g - 1], keep1.at[g - 1], own1.at[g - 1], tot1.at[g - 1]

    def partial_sum(g, q, load):
        if g == 0:
            load.wait()
            return mm(acts[rows256(q), :], signs[...])
        return mm(acts_pad[rows256(q), :], wbuf[g - 1])

    def reduce_send(g, kind, to):
        sb, rb = bufs(g)[:2]
        send(sb.at[kind], rb.at[kind], (rs_ss, rs_rs, (g, kind,)), to)

    def reduce_got(g, kind):
        rb = bufs(g)[1]
        arrived(rb.at[kind], rs_rs, (g, kind,))

    def reduce_0(g):
        sb = bufs(g)[0]
        part = partial_sum(g, opp, act_loads[0])
        sb[A_] = part[:128].astype(BF16)
        sb[B_] = part[128:].astype(BF16)

    def reduce_1(g):
        sb, rb, keep, own, tot = bufs(g)
        reduce_send(g, A_, to_right)
        reduce_send(g, B_, to_left)
        part = partial_sum(g, right, act_loads[1])
        sb[C_] = part[128:].astype(BF16)
        reduce_send(g, C_, to_right)
        keep[0] = part[:128]
        part = partial_sum(g, left, act_loads[2])
        sb[D_] = part[:128].astype(BF16)
        reduce_send(g, D_, to_left)
        keep[1] = part[128:]
        own[...] = partial_sum(g, x, act_loads[3])

    def reduce_2(g):
        sb, rb, keep, own, tot = bufs(g)
        reduce_got(g, A_)
        sb[E_] = (keep[0] + rb[A_].astype(F32)).astype(BF16)
        reduce_send(g, E_, to_right)
        reduce_got(g, B_)
        sb[F_] = (keep[1] + rb[B_].astype(F32)).astype(BF16)
        reduce_send(g, F_, to_left)

    def reduce_3(g):
        sb, rb, keep, own, tot = bufs(g)
        for kind in (C_, D_, E_, F_):
            reduce_got(g, kind)
        tot[0:128, :] = own[0:128, :] + rb[E_].astype(F32) + rb[D_].astype(F32)
        tot[128:256, :] = own[128:256, :] + rb[C_].astype(F32) + rb[F_].astype(F32)
        if g == 0:
            for j in range(NJ):
                swap_out[0, j] = tot[:, j * W : (j + 1) * W].astype(BF16)
        else:
            swap_out[1, g - 1] = tot[...].astype(BF16)
            swap(1, g - 1)

    def swap(k, j):
        send(swap_out.at[k, j], swap_in.at[k, j], (sw_ss, sw_rs, (k, j)), to_zh)

    def swapped(k, j, own):
        arrived(swap_in.at[k, j], sw_rs, (k, j))
        return own + swap_in[k, j].astype(F32)

    def signal_send(j, q, h, idx, to):
        rows = pl.ds(pl.multiple_of(q * 256 + h * 128, 128), 128)
        send(sig.at[j, rows], sig.at[j, rows], (ag_ss, ag_rs, (j, idx)), to)

    def signal_got(j, idx):
        arrived(sig.at[j, pl.ds(0, 128)], ag_rs, (j, idx))

    def signal_a(j):
        cols = slice(j * W, (j + 1) * W)
        probed = swapped(0, j, tot0[:, cols])
        out = swapped(1, j, tot1[j])
        slope = jnp.tanh(out - targets[:, cols].astype(F32))
        bend = (1.0 - slope * slope) * probed
        sig[j, rows256(x), 0:W] = (slope * inverse).astype(BF16)
        sig[j, rows256(x), W : 2 * W] = (bend * inverse).astype(BF16)
        signal_send(j, x, 0, 0, to_right)
        signal_send(j, x, 1, 3, to_left)
        signal_send(j, x, 1, 1, to_right)
        signal_send(j, x, 0, 2, to_left)

    def signal_c(j):
        signal_got(j, 0)
        signal_send(j, left, 0, 4, to_right)
        signal_got(j, 3)
        signal_send(j, right, 1, 5, to_left)

    def signal_d(j):
        for idx in (1, 2, 4, 5):
            signal_got(j, idx)

    def contract(rows, j):
        return lax.dot_general(
            acts_pad[:, rows], sig[j], (((0,), (0,)), ((), ())), preferred_element_type=F32
        )

    def terms_core(j):
        dsend[j] = contract(pl.ds(pl.multiple_of((1 - c) * 512, 512), 512), j).astype(BF16)
        send(dsend.at[j], drecv.at[j], (d_ss, d_rs, (j,)), to_core)
        town[j] = contract(pl.ds(own512, 512), j).reshape(8, 4, 16, 2 * W)

    def bulk_send(j, phase, pairs, whole):
        for src, dst, to in pairs:
            rcopy(src, dst, t_ss.at[j, phase], t_rs.at[j, phase], to).start()
        bulk.append((whole, t_ss, (j, phase)))

    def terms_1(j):
        arrived(drecv.at[j], d_rs, (j,))
        total = town[j] + drecv[j].astype(F32).reshape(8, 4, 16, 2 * W)
        town[j] = total
        tsend[j, 0] = total[..., :W].astype(BF16)
        tsend[j, 1] = total[..., W:].astype(BF16)
        bulk_send(
            j, 1,
            [(tsend.at[j, 1, :, (zl + 1 + i) % 4], recv_b1.at[j, i], to_zl[i]) for i in range(3)],
            recv_b1.at[j],
        )
        bulk_send(
            j, 0,
            [(tsend.at[j, 0, (y + 1 + i) % 8], recv_a1.at[j, i], to_y[i]) for i in range(7)],
            recv_a1.at[j],
        )

    def terms_2a(j):
        arrived(recv_a1.at[j], t_rs, (j, 0))
        total = town[j, y, :, :, 0:W]
        for i in range(7):
            total = total + recv_a1[j, i].astype(F32)
        sum_a[j] = total
        send_a2[j] = total.astype(BF16)
        bulk_send(
            j, 2,
            [(send_a2.at[j, (zl + 1 + i) % 4], recv_a2.at[j, i], to_zl[i]) for i in range(3)],
            recv_a2.at[j],
        )

    def terms_2b(j):
        arrived(recv_b1.at[j], t_rs, (j, 1))
        total = town[j, :, zl, :, W : 2 * W]
        for i in range(3):
            total = total + recv_b1[j, i].astype(F32)
        sum_b[j] = total
        send_b2[j] = total.astype(BF16)
        bulk_send(
            j, 3,
            [(send_b2.at[j, (y + 1 + i) % 8], recv_b2.at[j, i], to_y[i]) for i in range(7)],
            recv_b2.at[j],
        )

    def update(j):
        arrived(recv_a2.at[j], t_rs, (j, 2))
        grad = sum_a[j, zl]
        for i in range(3):
            grad = grad + recv_a2[j, i].astype(F32)
        arrived(recv_b2.at[j], t_rs, (j, 3))
        hvp = sum_b[j, y]
        for i in range(7):
            hvp = hvp + recv_b2[j, i].astype(F32)
        cols = slice(j * W, (j + 1) * W)
        estimate = signs16[:, cols] * hvp
        moment = 0.9 * moment16[:, cols] + 0.1 * grad
        curv = 0.9 * curv16[:, cols] + 0.1 * estimate
        moment_out[:, cols] = moment[0:14]
        curv_out[:, cols] = curv[0:14]
        step = jnp.clip(moment / jnp.maximum(0.05 * curv, 0.02), -1.0, 1.0)
        master = master16[:, cols]
        updated = master - 0.02 * (step + 0.1 * master)
        real = lax.broadcasted_iota(jnp.int32, updated.shape, 0) < 14
        nbuf[j, pl.ds(own16, 16), :] = jnp.where(real, updated, 0.0).astype(BF16)
        gather_all(nbuf, 1, j)

    stores = []

    def finish(j):
        gathered(nbuf, 1, j)
        obuf[j] = mm(sel_t[...], nbuf[j]).astype(BF16)
        store = pltpu.make_async_copy(
            obuf.at[j], new_hbm.at[:, pl.ds(j * W, W)], local_sem.at[6 + j]
        )
        store.start()
        stores.append(store)

    def source(p):
        r = p % 16
        row = (((p // 64) % 8) * 8 + ((p // 16) % 4) * 2 + p // 512) * 14 + r
        return jnp.where(r < 14, row, -1)

    def make_signs():
        probe_load.wait()
        signs[...] = (2 * probe[...] - 1).astype(F32).astype(BF16)

    def make_sel_t():
        @pl.loop(0, 7)
        def _(t):
            rows = pl.ds(pl.multiple_of(t * 128, 128), 128)
            k = lax.broadcasted_iota(jnp.int32, (128, 1024), 0) + t * 128
            p = source(lax.broadcasted_iota(jnp.int32, (1, 1024), 1))
            sel_t[rows, :] = jnp.where(k == p, 1.0, 0.0).astype(BF16)

    def make_acts_pad(first, last):
        @pl.loop(first, last)
        def _(t):
            rows = pl.ds(pl.multiple_of(t * 256, 256), 256)
            acts_pad[rows, :] = mm(acts[rows, :], sel_t[...]).astype(BF16)

    def make_signs16():
        p = source(lax.broadcasted_iota(jnp.int32, (16, 1), 0) + own16)
        k = lax.broadcasted_iota(jnp.int32, (16, 896), 1)
        signs16[...] = mm(jnp.where(k == p, 1.0, 0.0).astype(BF16), signs[...])

    steps = [
        (load_rows,), (make_signs,), (reduce_0, 0), (meet,),
        (gather_all, wbuf, 0, 0), (reduce_1, 0), (gather_all, wbuf, 0, 1),
        (make_sel_t,), (make_acts_pad, 0, 2), (reduce_2, 0), (make_acts_pad, 2, 4),
        (gather_all, wbuf, 0, 2), (gather_core, wbuf, 0, 0), (reduce_3, 0), (swap, 0, 0),
        (swap, 0, 1), (gathered, wbuf, 0, 0), (reduce_0, 1), (reduce_1, 1),
        (gather_core, wbuf, 0, 1), (reduce_2, 1), (gathered, wbuf, 0, 1), (reduce_0, 2),
        (reduce_1, 2), (reduce_3, 1), (gather_core, wbuf, 0, 2), (gathered, wbuf, 0, 2),
        (reduce_2, 2), (swap, 0, 2), (reduce_0, 3), (reduce_1, 3), (reduce_3, 2),
        (reduce_2, 3), (make_signs16,), (target_load.wait,), (signal_a, 0), (reduce_3, 3),
        (signal_c, 0), (signal_a, 1), (signal_d, 0), (terms_core, 0), (signal_c, 1),
        (terms_1, 0), (signal_a, 2), (signal_d, 1), (terms_core, 1), (signal_c, 2),
        (terms_1, 1), (terms_2b, 0), (terms_2a, 0), (signal_d, 2), (terms_core, 2),
        (terms_1, 2), (terms_2a, 1), (terms_2b, 1), (update, 0), (terms_2b, 2), (terms_2a, 2),
        (update, 1), (update, 2), (gather_core, nbuf, 1, 0), (gather_core, nbuf, 1, 1),
        (finish, 0), (gather_core, nbuf, 1, 2), (finish, 1), (finish, 2),
    ]
    for step, *values in steps:
        step(*values)
    for store in stores:
        store.wait()
    for copy in sent:
        copy.wait_send()
    for ref, ss, at in bulk:
        rcopy(ref, ref, ss.at[at], ss.at[at], to_core).wait_send()


def copy_kernel(*refs):
    count = len(refs) // 2
    for n in range(count):
        refs[count + n][...] = refs[n][...]


def body(acts, targets, probe, master, moment, curv):
    any_spec = pl.BlockSpec(memory_space=pl.ANY)
    vmem_spec = pl.BlockSpec(memory_space=pltpu.VMEM)
    dma = pltpu.SemaphoreType.DMA
    vm = pltpu.VMEM
    shapes = (
        jax.ShapeDtypeStruct((896, 384), BF16),
        jax.ShapeDtypeStruct((14, 384), F32),
        jax.ShapeDtypeStruct((14, 384), F32),
    )
    results = pl.pallas_call(
        kernel,
        out_shape=shapes,
        in_specs=[any_spec, any_spec, any_spec, vmem_spec, vmem_spec, vmem_spec],
        out_specs=(any_spec, vmem_spec, vmem_spec),
        scratch_shapes=[
            vm((1024, 896), BF16), vm((896, 384), jnp.int32), vm((256, 384), BF16),
            vm((896, 384), BF16), vm((1024, 1024), BF16), vm((896, 1024), BF16),
            vm((16, 384), F32), vm((16, 384), F32), vm((16, 384), F32), vm((16, 384), F32),
            vm((NJ, 1024, W), BF16), vm((NJ, 1024, W), BF16),
            vm((NJ, 1024, 2 * W), BF16), vm((NJ, 896, W), BF16),
            vm((6, 128, 384), BF16), vm((6, 128, 384), BF16),
            vm((NJ, 6, 128, W), BF16), vm((NJ, 6, 128, W), BF16),
            vm((2, 128, 384), F32), vm((256, 384), F32),
            vm((NJ, 2, 128, W), F32), vm((NJ, 256, W), F32),
            vm((256, 384), F32), vm((NJ, 256, W), F32),
            vm((2, NJ, 256, W), BF16), vm((2, NJ, 256, W), BF16),
            vm((NJ, 512, 2 * W), BF16), vm((NJ, 512, 2 * W), BF16), vm((NJ, 8, 4, 16, 2 * W), F32),
            vm((NJ, 2, 8, 4, 16, W), BF16), vm((NJ, 7, 4, 16, W), BF16), vm((NJ, 3, 8, 16, W), BF16),
            vm((NJ, 4, 16, W), F32), vm((NJ, 8, 16, W), F32),
            vm((NJ, 4, 16, W), BF16), vm((NJ, 8, 16, W), BF16),
            vm((NJ, 3, 16, W), BF16), vm((NJ, 7, 16, W), BF16),
            dma((9,)), dma((4, 6)), dma((4, 6)), dma((2, NJ)), dma((2, NJ)), dma((NJ, 6)), dma((NJ, 6)),
            dma((2, NJ)), dma((2, NJ)), dma((2, NJ)), dma((2, NJ)),
            dma((NJ,)), dma((NJ,)), dma((NJ, 4)), dma((NJ, 4)),
        ],
        compiler_params=pltpu.CompilerParams(
            collective_id=0, has_side_effects=True, vmem_limit_bytes=56 * 2**20
        ),
        name="sophia",
    )(acts, targets, probe, master, moment, curv)
    return pl.pallas_call(
        copy_kernel,
        out_shape=shapes,
        in_specs=[vmem_spec] * 3,
        out_specs=(vmem_spec,) * 3,
        name="write_out",
    )(*results)


def solution(mesh):
    in_specs = (
        P("dp", "tensor"),
        P("dp", None),
        P("tensor", None),
        P(("tensor", "dp"), None),
        P(("tensor", "dp"), None),
        P(("tensor", "dp"), None),
    )
    out_specs = (P("tensor", None), P(("tensor", "dp"), None), P(("tensor", "dp"), None))
    return jax.shard_map(body, mesh=mesh, in_specs=in_specs, out_specs=out_specs, check_vma=False)
```

```python
import math

import jax
import jax.numpy as jnp
from jax import lax
from jax.experimental import pallas as pl
from jax.experimental.pallas import tpu as pltpu
from jax.sharding import PartitionSpec as P

MESH = pl.DeviceIdType.MESH
F32 = jnp.float32
BF16 = jnp.bfloat16
NJ = 3
W = 128
A_, B_, C_, D_, E_, F_ = range(6)


def mm(a, b):
    return lax.dot_general(a, b, (((1,), (0,)), ((), ())), preferred_element_type=F32)


def mm_t(a, b):
    return lax.dot_general(a, b, (((1,), (1,)), ((), ())), preferred_element_type=F32)


def kernel(
    acts_hbm, targets_hbm, probe_hbm, master_ref, moment_ref, curv_ref,
    new_hbm, moment_out, curv_out,
    acts, probe, targets, signs, acts_pad, sel_t,
    master16, moment16, curv16, signs16,
    wbuf, nbuf, sig, obuf,
    s0, r0, s1, r1, keep0, own0, keep1, own1, tot0, tot1, swap_out, swap_in,
    dsend, drecv, town, tsend, recv_a1, recv_b1, sum_a, sum_b, send_a2, send_b2, recv_a2, recv_b2,
    local_sem, rs_ss, rs_rs, sw_ss, sw_rs, ag_ss, ag_rs,
    wa_ss, wa_rs, wc_ss, wc_rs, d_ss, d_rs, t_ss, t_rs,
):
    inverse = 1.0 / math.sqrt(acts_hbm.shape[0] * lax.axis_size("dp"))
    dp = lax.axis_index("dp")
    tensor = lax.axis_index("tensor")
    y, zl, c = dp // 8, (dp // 2) % 4, dp % 2
    zh, x = tensor // 4, tensor % 4
    right, left, opp = (x + 1) % 4, (x + 3) % 4, (x + 2) % 4

    def dev(y_=None, zl_=None, c_=None, zh_=None, x_=None):
        y_ = y if y_ is None else y_
        zl_ = zl if zl_ is None else zl_
        c_ = c if c_ is None else c_
        zh_ = zh if zh_ is None else zh_
        x_ = x if x_ is None else x_
        return (y_ * 8 + zl_ * 2 + c_, zh_ * 4 + x_)

    to_right, to_left = dev(x_=right), dev(x_=left)
    to_zh, to_core = dev(zh_=1 - zh), dev(c_=1 - c)
    to_zl = [dev(zl_=(zl + i) % 4) for i in range(1, 4)]
    to_y = [dev(y_=(y + i) % 8) for i in range(1, 8)]

    own16 = pl.multiple_of(c * 512 + y * 64 + zl * 16, 16)
    own512 = pl.multiple_of(c * 512, 512)

    def rcopy(src, dst, ss, rs, to):
        return pltpu.make_async_remote_copy(
            src_ref=src, dst_ref=dst, send_sem=ss, recv_sem=rs, device_id=to, device_id_type=MESH
        )

    sent, bulk = [], []

    def send(src, dst, sems, to):
        ss, rs, at = sems
        copy = rcopy(src, dst, ss.at[at], rs.at[at], to)
        copy.start()
        sent.append(copy)

    def arrived(dst, rs, at):
        rcopy(dst, dst, rs.at[at], rs.at[at], to_core).wait_recv()

    def rows256(q):
        return pl.ds(pl.multiple_of(q * 256, 256), 256)

    loads = []
    probe_load = pltpu.make_async_copy(probe_hbm, probe, local_sem.at[0])
    probe_load.start()
    act_loads = []
    for n, q in enumerate((opp, right, left, x)):
        load = pltpu.make_async_copy(
            acts_hbm.at[rows256(q), :], acts.at[rows256(q), :], local_sem.at[1 + n]
        )
        load.start()
        act_loads.append(load)
    target_load = pltpu.make_async_copy(targets_hbm.at[rows256(x), :], targets, local_sem.at[5])
    target_load.start()

    barrier = pltpu.get_barrier_semaphore()
    partners = [to_right, to_left, to_zh, to_core] + to_zl + to_y
    for to in partners:
        pl.semaphore_signal(barrier, inc=1, device_id=to, device_id_type=MESH)

    def meet():
        pl.semaphore_wait(barrier, len(partners))

    def load_rows():
        for padded, ref in ((master16, master_ref), (moment16, moment_ref), (curv16, curv_ref)):
            padded[...] = jnp.zeros_like(padded)
            padded[0:14, :] = ref[...]
        low = master16[...].astype(BF16)
        for j in range(NJ):
            wbuf[j, c, y, zl] = low[:, j * W : (j + 1) * W]

    def spread(copies, whole, sems):
        ss, rs, at = sems
        for src, dst, to in copies:
            rcopy(src, dst, ss.at[at], rs.at[at], to).start()
        bulk.append((whole, ss, at))

    def gather_1(buf, k, j):
        own = buf.at[j, c, y, zl]
        peers = to_y if j == 1 else to_zl
        whole = buf.at[j, 0, 0:7, 0] if j == 1 else buf.at[j, 0, 0, 0:3]
        spread([(own, own, to) for to in peers], whole, (wa_ss, wa_rs, (k, j, 0)))

    def gather_2(buf, k, j):
        if j == 1:
            arrived(buf.at[j, 0, 0:7, 0], wa_rs, (k, j, 0))
            block, peers, whole = buf.at[j, c, :, zl], to_zl, buf.at[j, 0, :, 0:3]
        else:
            arrived(buf.at[j, 0, 0, 0:3], wa_rs, (k, j, 0))
            block, peers, whole = buf.at[j, c, y], to_y, buf.at[j, 0, 0:7]
        spread([(block, block, to) for to in peers], whole, (wa_ss, wa_rs, (k, j, 1)))

    def gather_core(buf, k, j):
        whole = buf.at[j, 0, :, 0:3] if j == 1 else buf.at[j, 0, 0:7]
        arrived(whole, wa_rs, (k, j, 1))
        send(buf.at[j, c], buf.at[j, c], (wc_ss, wc_rs, (k, j)), to_core)

    def gathered(buf, k, j):
        arrived(buf.at[j, 0], wc_rs, (k, j))

    def bufs(g):
        if g == 0:
            return s0, r0, keep0, own0, tot0
        return s1.at[g - 1], r1.at[g - 1], keep1.at[g - 1], own1.at[g - 1], tot1.at[g - 1]

    def partial_sum(g, q, load):
        if g == 0:
            load.wait()
            return mm(acts[rows256(q), :], signs[...])
        return mm(acts_pad[rows256(q), :], wbuf[g - 1].reshape(1024, W))

    def reduce_send(g, kind, to):
        sb, rb = bufs(g)[:2]
        send(sb.at[kind], rb.at[kind], (rs_ss, rs_rs, (g, kind,)), to)

    def reduce_got(g, kind):
        rb = bufs(g)[1]
        arrived(rb.at[kind], rs_rs, (g, kind,))

    def reduce_0(g):
        sb = bufs(g)[0]
        part = partial_sum(g, opp, act_loads[0])
        sb[A_] = part[:128].astype(BF16)
        sb[B_] = part[128:].astype(BF16)

    def reduce_1(g):
        sb, rb, keep, own, tot = bufs(g)
        reduce_send(g, A_, to_right)
        reduce_send(g, B_, to_left)
        part = partial_sum(g, right, act_loads[1])
        sb[C_] = part[128:].astype(BF16)
        reduce_send(g, C_, to_right)
        keep[0] = part[:128]
        part = partial_sum(g, left, act_loads[2])
        sb[D_] = part[:128].astype(BF16)
        reduce_send(g, D_, to_left)
        keep[1] = part[128:]
        own[...] = partial_sum(g, x, act_loads[3])

    def reduce_2(g):
        sb, rb, keep, own, tot = bufs(g)
        reduce_got(g, A_)
        sb[E_] = (keep[0] + rb[A_].astype(F32)).astype(BF16)
        reduce_send(g, E_, to_right)
        reduce_got(g, B_)
        sb[F_] = (keep[1] + rb[B_].astype(F32)).astype(BF16)
        reduce_send(g, F_, to_left)

    def reduce_3(g):
        sb, rb, keep, own, tot = bufs(g)
        for kind in (C_, D_, E_, F_):
            reduce_got(g, kind)
        tot[0:128, :] = own[0:128, :] + rb[E_].astype(F32) + rb[D_].astype(F32)
        tot[128:256, :] = own[128:256, :] + rb[C_].astype(F32) + rb[F_].astype(F32)
        if g == 0:
            for j in range(NJ):
                swap_out[0, j] = tot[:, j * W : (j + 1) * W].astype(BF16)
        else:
            swap_out[1, g - 1] = tot[...].astype(BF16)
            swap(1, g - 1)

    def swap(k, j):
        send(swap_out.at[k, j], swap_in.at[k, j], (sw_ss, sw_rs, (k, j)), to_zh)

    def swapped(k, j, own):
        arrived(swap_in.at[k, j], sw_rs, (k, j))
        return own + swap_in[k, j].astype(F32)

    def signal_send(j, q, h, idx, to):
        rows = pl.ds(pl.multiple_of(q * 256 + h * 128, 128), 128)
        send(sig.at[j, rows], sig.at[j, rows], (ag_ss, ag_rs, (j, idx)), to)

    def signal_got(j, idx):
        arrived(sig.at[j, pl.ds(0, 128)], ag_rs, (j, idx))

    def signal_a(j):
        cols = slice(j * W, (j + 1) * W)
        probed = swapped(0, j, tot0[:, cols])
        out = swapped(1, j, tot1[j])
        slope = jnp.tanh(out - targets[:, cols].astype(F32))
        bend = (1.0 - slope * slope) * probed
        sig[j, rows256(x), 0:W] = (slope * inverse).astype(BF16)
        sig[j, rows256(x), W : 2 * W] = (bend * inverse).astype(BF16)
        signal_send(j, x, 0, 0, to_right)
        signal_send(j, x, 1, 3, to_left)
        signal_send(j, x, 1, 1, to_right)
        signal_send(j, x, 0, 2, to_left)

    def signal_c(j):
        signal_got(j, 0)
        signal_send(j, left, 0, 4, to_right)
        signal_got(j, 3)
        signal_send(j, right, 1, 5, to_left)

    def signal_d(j):
        for idx in (1, 2, 4, 5):
            signal_got(j, idx)

    def contract(rows, j):
        return lax.dot_general(
            acts_pad[:, rows], sig[j], (((0,), (0,)), ((), ())), preferred_element_type=F32
        )

    def terms_core(j):
        dsend[j] = contract(pl.ds(pl.multiple_of((1 - c) * 512, 512), 512), j).astype(BF16)
        send(dsend.at[j], drecv.at[j], (d_ss, d_rs, (j,)), to_core)
        town[j] = contract(pl.ds(own512, 512), j).reshape(8, 4, 16, 2 * W)

    def terms_1(j):
        arrived(drecv.at[j], d_rs, (j,))
        total = town[j] + drecv[j].astype(F32).reshape(8, 4, 16, 2 * W)
        town[j] = total
        tsend[j, 0] = total[..., :W].astype(BF16)
        tsend[j, 1] = total[..., W:].astype(BF16)
        spread(
            [(tsend.at[j, 1, :, (zl + 1 + i) % 4], recv_b1.at[j, i], to_zl[i]) for i in range(3)],
            recv_b1.at[j], (t_ss, t_rs, (j, 1)),
        )
        spread(
            [(tsend.at[j, 0, (y + 1 + i) % 8], recv_a1.at[j, i], to_y[i]) for i in range(7)],
            recv_a1.at[j], (t_ss, t_rs, (j, 0)),
        )

    def terms_2a(j):
        arrived(recv_a1.at[j], t_rs, (j, 0))
        total = town[j, y, :, :, 0:W]
        for i in range(7):
            total = total + recv_a1[j, i].astype(F32)
        sum_a[j] = total
        send_a2[j] = total.astype(BF16)
        spread(
            [(send_a2.at[j, (zl + 1 + i) % 4], recv_a2.at[j, i], to_zl[i]) for i in range(3)],
            recv_a2.at[j], (t_ss, t_rs, (j, 2)),
        )

    def terms_2b(j):
        arrived(recv_b1.at[j], t_rs, (j, 1))
        total = town[j, :, zl, :, W : 2 * W]
        for i in range(3):
            total = total + recv_b1[j, i].astype(F32)
        sum_b[j] = total
        send_b2[j] = total.astype(BF16)
        spread(
            [(send_b2.at[j, (y + 1 + i) % 8], recv_b2.at[j, i], to_y[i]) for i in range(7)],
            recv_b2.at[j], (t_ss, t_rs, (j, 3)),
        )

    def update(j):
        arrived(recv_a2.at[j], t_rs, (j, 2))
        grad = sum_a[j, zl]
        for i in range(3):
            grad = grad + recv_a2[j, i].astype(F32)
        arrived(recv_b2.at[j], t_rs, (j, 3))
        hvp = sum_b[j, y]
        for i in range(7):
            hvp = hvp + recv_b2[j, i].astype(F32)
        cols = slice(j * W, (j + 1) * W)
        estimate = signs16[:, cols] * hvp
        moment = 0.9 * moment16[:, cols] + 0.1 * grad
        curv = 0.9 * curv16[:, cols] + 0.1 * estimate
        moment_out[:, cols] = moment[0:14]
        curv_out[:, cols] = curv[0:14]
        step = jnp.clip(moment / jnp.maximum(0.05 * curv, 0.02), -1.0, 1.0)
        master = master16[:, cols]
        updated = master - 0.02 * (step + 0.1 * master)
        real = lax.broadcasted_iota(jnp.int32, updated.shape, 0) < 14
        nbuf[j, c, y, zl] = jnp.where(real, updated, 0.0).astype(BF16)
        gather_1(nbuf, 1, j)

    stores = []

    def finish(j):
        gathered(nbuf, 1, j)
        obuf[j] = mm(sel_t[...], nbuf[j].reshape(1024, W)).astype(BF16)
        store = pltpu.make_async_copy(
            obuf.at[j], new_hbm.at[:, pl.ds(j * W, W)], local_sem.at[6 + j]
        )
        store.start()
        stores.append(store)

    def source(p):
        r = p % 16
        row = (((p // 64) % 8) * 8 + ((p // 16) % 4) * 2 + p // 512) * 14 + r
        return jnp.where(r < 14, row, -1)

    def make_signs():
        probe_load.wait()
        signs[...] = (2 * probe[...] - 1).astype(F32).astype(BF16)

    def make_sel_t():
        @pl.loop(0, 7)
        def _(t):
            rows = pl.ds(pl.multiple_of(t * 128, 128), 128)
            k = lax.broadcasted_iota(jnp.int32, (128, 1024), 0) + t * 128
            p = source(lax.broadcasted_iota(jnp.int32, (1, 1024), 1))
            sel_t[rows, :] = jnp.where(k == p, 1.0, 0.0).astype(BF16)

    def make_acts_pad(first, last):
        @pl.loop(first, last)
        def _(t):
            rows = pl.ds(pl.multiple_of(t * 256, 256), 256)
            acts_pad[rows, :] = mm(acts[rows, :], sel_t[...]).astype(BF16)

    def make_signs16():
        p = source(lax.broadcasted_iota(jnp.int32, (16, 1), 0) + own16)
        k = lax.broadcasted_iota(jnp.int32, (16, 896), 1)
        signs16[...] = mm(jnp.where(k == p, 1.0, 0.0).astype(BF16), signs[...])

    steps = [
        (load_rows,), (make_signs,), (reduce_0, 0), (meet,),
        (gather_1, wbuf, 0, 0), (gather_1, wbuf, 0, 1), (gather_1, wbuf, 0, 2), (reduce_1, 0),
        (gather_2, wbuf, 0, 0), (gather_2, wbuf, 0, 1), (reduce_2, 0), (gather_2, wbuf, 0, 2),
        (make_sel_t,), (make_acts_pad, 0, 4), (gather_core, wbuf, 0, 0), (reduce_3, 0),
        (gather_core, wbuf, 0, 1), (swap, 0, 0), (gathered, wbuf, 0, 0), (reduce_0, 1),
        (reduce_1, 1), (gather_core, wbuf, 0, 2), (gathered, wbuf, 0, 1), (swap, 0, 1),
        (reduce_0, 2), (reduce_1, 2), (reduce_2, 1), (gathered, wbuf, 0, 2), (reduce_2, 2),
        (reduce_3, 1), (reduce_0, 3), (reduce_1, 3), (reduce_3, 2), (swap, 0, 2),
        (reduce_2, 3), (make_signs16,), (target_load.wait,), (reduce_3, 3), (signal_a, 0),
        (signal_a, 1), (signal_c, 0), (signal_c, 1), (signal_a, 2), (signal_d, 0),
        (terms_core, 0), (signal_d, 1), (terms_core, 1), (signal_c, 2), (terms_1, 0),
        (terms_1, 1), (signal_d, 2), (terms_core, 2), (terms_1, 2), (terms_2b, 0),
        (terms_2a, 0), (terms_2b, 1), (terms_2a, 1), (terms_2b, 2), (terms_2a, 2),
        (update, 0), (update, 1), (update, 2), (gather_2, nbuf, 1, 0), (gather_2, nbuf, 1, 1),
        (gather_2, nbuf, 1, 2), (gather_core, nbuf, 1, 0), (gather_core, nbuf, 1, 1),
        (finish, 0), (gather_core, nbuf, 1, 2), (finish, 1), (finish, 2),
    ]
    for step, *values in steps:
        step(*values)
    for store in stores:
        store.wait()
    for copy in sent:
        copy.wait_send()
    for ref, ss, at in bulk:
        rcopy(ref, ref, ss.at[at], ss.at[at], to_core).wait_send()


def copy_kernel(*refs):
    count = len(refs) // 2
    for n in range(count):
        refs[count + n][...] = refs[n][...]


def body(acts, targets, probe, master, moment, curv):
    any_spec = pl.BlockSpec(memory_space=pl.ANY)
    vmem_spec = pl.BlockSpec(memory_space=pltpu.VMEM)
    dma = pltpu.SemaphoreType.DMA
    vm = pltpu.VMEM
    shapes = (
        jax.ShapeDtypeStruct((896, 384), BF16),
        jax.ShapeDtypeStruct((14, 384), F32),
        jax.ShapeDtypeStruct((14, 384), F32),
    )
    results = pl.pallas_call(
        kernel,
        out_shape=shapes,
        in_specs=[any_spec, any_spec, any_spec, vmem_spec, vmem_spec, vmem_spec],
        out_specs=(any_spec, vmem_spec, vmem_spec),
        scratch_shapes=[
            vm((1024, 896), BF16), vm((896, 384), jnp.int32), vm((256, 384), BF16),
            vm((896, 384), BF16), vm((1024, 1024), BF16), vm((896, 1024), BF16),
            vm((16, 384), F32), vm((16, 384), F32), vm((16, 384), F32), vm((16, 384), F32),
            vm((NJ, 2, 8, 4, 16, W), BF16), vm((NJ, 2, 8, 4, 16, W), BF16),
            vm((NJ, 1024, 2 * W), BF16), vm((NJ, 896, W), BF16),
            vm((6, 128, 384), BF16), vm((6, 128, 384), BF16),
            vm((NJ, 6, 128, W), BF16), vm((NJ, 6, 128, W), BF16),
            vm((2, 128, 384), F32), vm((256, 384), F32),
            vm((NJ, 2, 128, W), F32), vm((NJ, 256, W), F32),
            vm((256, 384), F32), vm((NJ, 256, W), F32),
            vm((2, NJ, 256, W), BF16), vm((2, NJ, 256, W), BF16),
            vm((NJ, 512, 2 * W), BF16), vm((NJ, 512, 2 * W), BF16), vm((NJ, 8, 4, 16, 2 * W), F32),
            vm((NJ, 2, 8, 4, 16, W), BF16), vm((NJ, 7, 4, 16, W), BF16), vm((NJ, 3, 8, 16, W), BF16),
            vm((NJ, 4, 16, W), F32), vm((NJ, 8, 16, W), F32),
            vm((NJ, 4, 16, W), BF16), vm((NJ, 8, 16, W), BF16),
            vm((NJ, 3, 16, W), BF16), vm((NJ, 7, 16, W), BF16),
            dma((9,)), dma((4, 6)), dma((4, 6)), dma((2, NJ)), dma((2, NJ)), dma((NJ, 6)), dma((NJ, 6)),
            dma((2, NJ, 2)), dma((2, NJ, 2)), dma((2, NJ)), dma((2, NJ)),
            dma((NJ,)), dma((NJ,)), dma((NJ, 4)), dma((NJ, 4)),
        ],
        compiler_params=pltpu.CompilerParams(
            collective_id=0, has_side_effects=True, vmem_limit_bytes=56 * 2**20
        ),
        name="sophia",
    )(acts, targets, probe, master, moment, curv)
    return pl.pallas_call(
        copy_kernel,
        out_shape=shapes,
        in_specs=[vmem_spec] * 3,
        out_specs=(vmem_spec,) * 3,
        name="write_out",
    )(*results)


def solution(mesh):
    in_specs = (
        P("dp", "tensor"),
        P("dp", None),
        P("tensor", None),
        P(("tensor", "dp"), None),
        P(("tensor", "dp"), None),
        P(("tensor", "dp"), None),
    )
    out_specs = (P("tensor", None), P(("tensor", "dp"), None), P(("tensor", "dp"), None))
    return jax.shard_map(body, mesh=mesh, in_specs=in_specs, out_specs=out_specs, check_vma=False)
```

```python
import math

import jax
import jax.numpy as jnp
from jax import lax
from jax.experimental import pallas as pl
from jax.experimental.pallas import tpu as pltpu
from jax.sharding import PartitionSpec as P

MESH = pl.DeviceIdType.MESH
F32 = jnp.float32
BF16 = jnp.bfloat16
NJ = 3
W = 128
A_, B_, C_, D_, E_, F_ = range(6)


def mm(a, b):
    return lax.dot_general(a, b, (((1,), (0,)), ((), ())), preferred_element_type=F32)


def mm_t(a, b):
    return lax.dot_general(a, b, (((1,), (1,)), ((), ())), preferred_element_type=F32)


def kernel(
    acts_hbm, targets_hbm, probe_hbm, master_hbm, moment_hbm, curv_hbm,
    new_hbm, moment_hbm_out, curv_hbm_out,
    master_in, moment_in, curv_in, moment_out, curv_out,
    acts, probe, targets, signs, acts_pad, sel_t,
    master16, moment16, curv16, signs16,
    wbuf, nbuf, sig, obuf,
    s0, r0, s1, r1, keep0, own0, keep1, own1, tot0, tot1, swap_out, swap_in,
    dsend, drecv, town, tsend, recv_a1, recv_b1, sum_a, sum_b, send_a2, send_b2, recv_a2, recv_b2,
    local_sem, rs_ss, rs_rs, sw_ss, sw_rs, ag_ss, ag_rs,
    wa_ss, wa_rs, wc_ss, wc_rs, d_ss, d_rs, t_ss, t_rs,
):
    inverse = 1.0 / math.sqrt(acts_hbm.shape[0] * lax.axis_size("dp"))
    dp = lax.axis_index("dp")
    tensor = lax.axis_index("tensor")
    y, zl, c = dp // 8, (dp // 2) % 4, dp % 2
    zh, x = tensor // 4, tensor % 4
    right, left, opp = (x + 1) % 4, (x + 3) % 4, (x + 2) % 4

    def dev(y_=None, zl_=None, c_=None, zh_=None, x_=None):
        y_ = y if y_ is None else y_
        zl_ = zl if zl_ is None else zl_
        c_ = c if c_ is None else c_
        zh_ = zh if zh_ is None else zh_
        x_ = x if x_ is None else x_
        return (y_ * 8 + zl_ * 2 + c_, zh_ * 4 + x_)

    to_right, to_left = dev(x_=right), dev(x_=left)
    to_zh, to_core = dev(zh_=1 - zh), dev(c_=1 - c)
    to_zl = [dev(zl_=(zl + i) % 4) for i in range(1, 4)]
    to_y = [dev(y_=(y + i) % 8) for i in range(1, 8)]

    own16 = pl.multiple_of(c * 512 + y * 64 + zl * 16, 16)
    own512 = pl.multiple_of(c * 512, 512)

    def rcopy(src, dst, ss, rs, to):
        return pltpu.make_async_remote_copy(
            src_ref=src, dst_ref=dst, send_sem=ss, recv_sem=rs, device_id=to, device_id_type=MESH
        )

    sent, bulk = [], []

    def send(src, dst, sems, to):
        ss, rs, at = sems
        copy = rcopy(src, dst, ss.at[at], rs.at[at], to)
        copy.start()
        sent.append(copy)

    def arrived(dst, rs, at):
        rcopy(dst, dst, rs.at[at], rs.at[at], to_core).wait_recv()

    def rows256(q):
        return pl.ds(pl.multiple_of(q * 256, 256), 256)

    barrier = pltpu.get_barrier_semaphore()
    partners = [to_right, to_left, to_zh, to_core] + to_zl + to_y
    for to in partners:
        pl.semaphore_signal(barrier, inc=1, device_id=to, device_id_type=MESH)

    state_loads = []
    for n, (src, dst) in enumerate(
        ((master_hbm, master_in), (moment_hbm, moment_in), (curv_hbm, curv_in))
    ):
        load = pltpu.make_async_copy(src, dst, local_sem.at[9 + n])
        load.start()
        state_loads.append(load)
    probe_load = pltpu.make_async_copy(probe_hbm, probe, local_sem.at[0])
    probe_load.start()
    act_loads = []
    for n, q in enumerate((opp, right, left, x)):
        load = pltpu.make_async_copy(
            acts_hbm.at[rows256(q), :], acts.at[rows256(q), :], local_sem.at[1 + n]
        )
        load.start()
        act_loads.append(load)
    target_load = pltpu.make_async_copy(targets_hbm.at[rows256(x), :], targets, local_sem.at[5])
    target_load.start()

    def meet():
        pl.semaphore_wait(barrier, len(partners))

    def load_rows():
        state_loads[0].wait()
        master16[...] = jnp.zeros_like(master16)
        master16[0:14, :] = master_in[...]
        low = master16[...].astype(BF16)
        for j in range(NJ):
            wbuf[j, c, y, zl] = low[:, j * W : (j + 1) * W]

    def load_states():
        for n, (padded, ref) in enumerate(((moment16, moment_in), (curv16, curv_in))):
            state_loads[1 + n].wait()
            padded[...] = jnp.zeros_like(padded)
            padded[0:14, :] = ref[...]

    def spread(copies, whole, sems):
        ss, rs, at = sems
        for src, dst, to in copies:
            rcopy(src, dst, ss.at[at], rs.at[at], to).start()
        bulk.append((whole, ss, at))

    def gather_1(buf, k, j):
        own = buf.at[j, c, y, zl]
        peers = to_y if j == 1 else to_zl
        whole = buf.at[j, 0, 0:7, 0] if j == 1 else buf.at[j, 0, 0, 0:3]
        spread([(own, own, to) for to in peers], whole, (wa_ss, wa_rs, (k, j, 0)))

    def gather_2(buf, k, j):
        if j == 1:
            arrived(buf.at[j, 0, 0:7, 0], wa_rs, (k, j, 0))
            block, peers, whole = buf.at[j, c, :, zl], to_zl, buf.at[j, 0, :, 0:3]
        else:
            arrived(buf.at[j, 0, 0, 0:3], wa_rs, (k, j, 0))
            block, peers, whole = buf.at[j, c, y], to_y, buf.at[j, 0, 0:7]
        spread([(block, block, to) for to in peers], whole, (wa_ss, wa_rs, (k, j, 1)))

    def gather_core(buf, k, j):
        whole = buf.at[j, 0, :, 0:3] if j == 1 else buf.at[j, 0, 0:7]
        arrived(whole, wa_rs, (k, j, 1))
        send(buf.at[j, c], buf.at[j, c], (wc_ss, wc_rs, (k, j)), to_core)

    def gathered(buf, k, j):
        arrived(buf.at[j, 0], wc_rs, (k, j))

    def bufs(g):
        if g == 0:
            return s0, r0, keep0, own0, tot0
        return s1.at[g - 1], r1.at[g - 1], keep1.at[g - 1], own1.at[g - 1], tot1.at[g - 1]

    def partial_sum(g, q, load):
        if g == 0:
            load.wait()
            return mm(acts[rows256(q), :], signs[...])
        return mm(acts_pad[rows256(q), :], wbuf[g - 1].reshape(1024, W))

    def reduce_send(g, kind, to):
        sb, rb = bufs(g)[:2]
        send(sb.at[kind], rb.at[kind], (rs_ss, rs_rs, (g, kind,)), to)

    def reduce_got(g, kind):
        rb = bufs(g)[1]
        arrived(rb.at[kind], rs_rs, (g, kind,))

    def reduce_0(g):
        sb = bufs(g)[0]
        part = partial_sum(g, opp, act_loads[0])
        sb[A_] = part[:128].astype(BF16)
        sb[B_] = part[128:].astype(BF16)

    def reduce_1(g):
        sb, rb, keep, own, tot = bufs(g)
        reduce_send(g, A_, to_right)
        reduce_send(g, B_, to_left)
        part = partial_sum(g, right, act_loads[1])
        sb[C_] = part[128:].astype(BF16)
        reduce_send(g, C_, to_right)
        keep[0] = part[:128]
        part = partial_sum(g, left, act_loads[2])
        sb[D_] = part[:128].astype(BF16)
        reduce_send(g, D_, to_left)
        keep[1] = part[128:]
        own[...] = partial_sum(g, x, act_loads[3])

    def reduce_2(g):
        sb, rb, keep, own, tot = bufs(g)
        reduce_got(g, A_)
        sb[E_] = (keep[0] + rb[A_].astype(F32)).astype(BF16)
        reduce_send(g, E_, to_right)
        reduce_got(g, B_)
        sb[F_] = (keep[1] + rb[B_].astype(F32)).astype(BF16)
        reduce_send(g, F_, to_left)

    def reduce_3(g):
        sb, rb, keep, own, tot = bufs(g)
        for kind in (C_, D_, E_, F_):
            reduce_got(g, kind)
        tot[0:128, :] = own[0:128, :] + rb[E_].astype(F32) + rb[D_].astype(F32)
        tot[128:256, :] = own[128:256, :] + rb[C_].astype(F32) + rb[F_].astype(F32)
        if g == 0:
            for j in range(NJ):
                swap_out[0, j] = tot[:, j * W : (j + 1) * W].astype(BF16)
        else:
            swap_out[1, g - 1] = tot[...].astype(BF16)
            swap(1, g - 1)

    def swap(k, j):
        send(swap_out.at[k, j], swap_in.at[k, j], (sw_ss, sw_rs, (k, j)), to_zh)

    def swapped(k, j, own):
        arrived(swap_in.at[k, j], sw_rs, (k, j))
        return own + swap_in[k, j].astype(F32)

    def signal_send(j, q, h, idx, to):
        rows = pl.ds(pl.multiple_of(q * 256 + h * 128, 128), 128)
        send(sig.at[j, rows], sig.at[j, rows], (ag_ss, ag_rs, (j, idx)), to)

    def signal_got(j, idx):
        arrived(sig.at[j, pl.ds(0, 128)], ag_rs, (j, idx))

    def signal_a(j):
        cols = slice(j * W, (j + 1) * W)
        probed = swapped(0, j, tot0[:, cols])
        out = swapped(1, j, tot1[j])
        slope = jnp.tanh(out - targets[:, cols].astype(F32))
        bend = (1.0 - slope * slope) * probed
        sig[j, rows256(x), 0:W] = (slope * inverse).astype(BF16)
        sig[j, rows256(x), W : 2 * W] = (bend * inverse).astype(BF16)
        signal_send(j, x, 0, 0, to_right)
        signal_send(j, x, 1, 3, to_left)
        signal_send(j, x, 1, 1, to_right)
        signal_send(j, x, 0, 2, to_left)

    def signal_c(j):
        signal_got(j, 0)
        signal_send(j, left, 0, 4, to_right)
        signal_got(j, 3)
        signal_send(j, right, 1, 5, to_left)

    def signal_d(j):
        for idx in (1, 2, 4, 5):
            signal_got(j, idx)

    def contract(rows, j):
        return lax.dot_general(
            acts_pad[:, rows], sig[j], (((0,), (0,)), ((), ())), preferred_element_type=F32
        )

    def terms_core(j):
        dsend[j] = contract(pl.ds(pl.multiple_of((1 - c) * 512, 512), 512), j).astype(BF16)
        send(dsend.at[j], drecv.at[j], (d_ss, d_rs, (j,)), to_core)
        town[j] = contract(pl.ds(own512, 512), j).reshape(8, 4, 16, 2 * W)

    def terms_1(j):
        arrived(drecv.at[j], d_rs, (j,))
        total = town[j] + drecv[j].astype(F32).reshape(8, 4, 16, 2 * W)
        town[j] = total
        tsend[j, 0] = total[..., :W].astype(BF16)
        tsend[j, 1] = total[..., W:].astype(BF16)
        spread(
            [(tsend.at[j, 1, :, (zl + 1 + i) % 4], recv_b1.at[j, i], to_zl[i]) for i in range(3)],
            recv_b1.at[j], (t_ss, t_rs, (j, 1)),
        )
        spread(
            [(tsend.at[j, 0, (y + 1 + i) % 8], recv_a1.at[j, i], to_y[i]) for i in range(7)],
            recv_a1.at[j], (t_ss, t_rs, (j, 0)),
        )

    def terms_2a(j):
        arrived(recv_a1.at[j], t_rs, (j, 0))
        total = town[j, y, :, :, 0:W]
        for i in range(7):
            total = total + recv_a1[j, i].astype(F32)
        sum_a[j] = total
        send_a2[j] = total.astype(BF16)
        spread(
            [(send_a2.at[j, (zl + 1 + i) % 4], recv_a2.at[j, i], to_zl[i]) for i in range(3)],
            recv_a2.at[j], (t_ss, t_rs, (j, 2)),
        )

    def terms_2b(j):
        arrived(recv_b1.at[j], t_rs, (j, 1))
        total = town[j, :, zl, :, W : 2 * W]
        for i in range(3):
            total = total + recv_b1[j, i].astype(F32)
        sum_b[j] = total
        send_b2[j] = total.astype(BF16)
        spread(
            [(send_b2.at[j, (y + 1 + i) % 8], recv_b2.at[j, i], to_y[i]) for i in range(7)],
            recv_b2.at[j], (t_ss, t_rs, (j, 3)),
        )

    def update(j):
        arrived(recv_a2.at[j], t_rs, (j, 2))
        grad = sum_a[j, zl]
        for i in range(3):
            grad = grad + recv_a2[j, i].astype(F32)
        arrived(recv_b2.at[j], t_rs, (j, 3))
        hvp = sum_b[j, y]
        for i in range(7):
            hvp = hvp + recv_b2[j, i].astype(F32)
        cols = slice(j * W, (j + 1) * W)
        estimate = signs16[:, cols] * hvp
        moment = 0.9 * moment16[:, cols] + 0.1 * grad
        curv = 0.9 * curv16[:, cols] + 0.1 * estimate
        moment_out[:, cols] = moment[0:14]
        curv_out[:, cols] = curv[0:14]
        step = jnp.clip(moment / jnp.maximum(0.05 * curv, 0.02), -1.0, 1.0)
        master = master16[:, cols]
        updated = master - 0.02 * (step + 0.1 * master)
        real = lax.broadcasted_iota(jnp.int32, updated.shape, 0) < 14
        nbuf[j, c, y, zl] = jnp.where(real, updated, 0.0).astype(BF16)
        gather_1(nbuf, 1, j)

    stores = []

    def store_states():
        for n, (src, dst) in enumerate(((moment_out, moment_hbm_out), (curv_out, curv_hbm_out))):
            store = pltpu.make_async_copy(src, dst, local_sem.at[12 + n])
            store.start()
            stores.append(store)

    def finish(j):
        gathered(nbuf, 1, j)
        obuf[j] = mm(sel_t[...], nbuf[j].reshape(1024, W)).astype(BF16)
        store = pltpu.make_async_copy(
            obuf.at[j], new_hbm.at[:, pl.ds(j * W, W)], local_sem.at[6 + j]
        )
        store.start()
        stores.append(store)

    def source(p):
        r = p % 16
        row = (((p // 64) % 8) * 8 + ((p // 16) % 4) * 2 + p // 512) * 14 + r
        return jnp.where(r < 14, row, -1)

    def make_signs():
        probe_load.wait()
        signs[...] = (2 * probe[...] - 1).astype(F32).astype(BF16)

    def make_sel_t():
        @pl.loop(0, 7)
        def _(t):
            rows = pl.ds(pl.multiple_of(t * 128, 128), 128)
            k = lax.broadcasted_iota(jnp.int32, (128, 1024), 0) + t * 128
            p = source(lax.broadcasted_iota(jnp.int32, (1, 1024), 1))
            sel_t[rows, :] = jnp.where(k == p, 1.0, 0.0).astype(BF16)

    def make_acts_pad(first, last):
        @pl.loop(first, last)
        def _(t):
            rows = pl.ds(pl.multiple_of(t * 256, 256), 256)
            acts_pad[rows, :] = mm(acts[rows, :], sel_t[...]).astype(BF16)

    def make_signs16():
        p = source(lax.broadcasted_iota(jnp.int32, (16, 1), 0) + own16)
        k = lax.broadcasted_iota(jnp.int32, (16, 896), 1)
        signs16[...] = mm(jnp.where(k == p, 1.0, 0.0).astype(BF16), signs[...])

    steps = [
        (load_rows,), (meet,), (gather_1, wbuf, 0, 0), (gather_1, wbuf, 0, 1),
        (gather_1, wbuf, 0, 2), (make_signs,), (reduce_0, 0), (reduce_1, 0),
        (gather_2, wbuf, 0, 0), (gather_2, wbuf, 0, 1), (reduce_2, 0), (gather_2, wbuf, 0, 2),
        (make_sel_t,), (make_acts_pad, 0, 4), (gather_core, wbuf, 0, 0), (reduce_3, 0),
        (gather_core, wbuf, 0, 1), (swap, 0, 0), (gathered, wbuf, 0, 0), (reduce_0, 1),
        (reduce_1, 1), (gather_core, wbuf, 0, 2), (gathered, wbuf, 0, 1), (swap, 0, 1),
        (reduce_0, 2), (reduce_1, 2), (reduce_2, 1), (gathered, wbuf, 0, 2), (reduce_2, 2),
        (reduce_3, 1), (reduce_0, 3), (reduce_1, 3), (reduce_3, 2), (swap, 0, 2),
        (reduce_2, 3), (make_signs16,), (load_states,), (target_load.wait,), (reduce_3, 3), (signal_a, 0),
        (signal_a, 1), (signal_c, 0), (signal_c, 1), (signal_a, 2), (signal_d, 0),
        (terms_core, 0), (signal_d, 1), (terms_core, 1), (signal_c, 2), (terms_1, 0),
        (terms_1, 1), (signal_d, 2), (terms_core, 2), (terms_1, 2), (terms_2b, 0),
        (terms_2a, 0), (terms_2b, 1), (terms_2a, 1), (terms_2b, 2), (terms_2a, 2),
        (update, 0), (update, 1), (update, 2), (store_states,), (gather_2, nbuf, 1, 0), (gather_2, nbuf, 1, 1),
        (gather_2, nbuf, 1, 2), (gather_core, nbuf, 1, 0), (gather_core, nbuf, 1, 1),
        (finish, 0), (gather_core, nbuf, 1, 2), (finish, 1), (finish, 2),
    ]
    for step, *values in steps:
        step(*values)
    for store in stores:
        store.wait()
    for copy in sent:
        copy.wait_send()
    for ref, ss, at in bulk:
        rcopy(ref, ref, ss.at[at], ss.at[at], to_core).wait_send()


def copy_kernel(*refs):
    count = len(refs) // 2
    for n in range(count):
        refs[count + n][...] = refs[n][...]


def body(acts, targets, probe, master, moment, curv):
    any_spec = pl.BlockSpec(memory_space=pl.ANY)
    vmem_spec = pl.BlockSpec(memory_space=pltpu.VMEM)
    dma = pltpu.SemaphoreType.DMA
    vm = pltpu.VMEM
    shapes = (
        jax.ShapeDtypeStruct((896, 384), BF16),
        jax.ShapeDtypeStruct((14, 384), F32),
        jax.ShapeDtypeStruct((14, 384), F32),
    )
    results = pl.pallas_call(
        kernel,
        out_shape=shapes,
        in_specs=[any_spec] * 6,
        out_specs=(any_spec,) * 3,
        scratch_shapes=[
            vm((14, 384), F32), vm((14, 384), F32), vm((14, 384), F32), vm((14, 384), F32),
            vm((14, 384), F32),
            vm((1024, 896), BF16), vm((896, 384), jnp.int32), vm((256, 384), BF16),
            vm((896, 384), BF16), vm((1024, 1024), BF16), vm((896, 1024), BF16),
            vm((16, 384), F32), vm((16, 384), F32), vm((16, 384), F32), vm((16, 384), F32),
            vm((NJ, 2, 8, 4, 16, W), BF16), vm((NJ, 2, 8, 4, 16, W), BF16),
            vm((NJ, 1024, 2 * W), BF16), vm((NJ, 896, W), BF16),
            vm((6, 128, 384), BF16), vm((6, 128, 384), BF16),
            vm((NJ, 6, 128, W), BF16), vm((NJ, 6, 128, W), BF16),
            vm((2, 128, 384), F32), vm((256, 384), F32),
            vm((NJ, 2, 128, W), F32), vm((NJ, 256, W), F32),
            vm((256, 384), F32), vm((NJ, 256, W), F32),
            vm((2, NJ, 256, W), BF16), vm((2, NJ, 256, W), BF16),
            vm((NJ, 512, 2 * W), BF16), vm((NJ, 512, 2 * W), BF16), vm((NJ, 8, 4, 16, 2 * W), F32),
            vm((NJ, 2, 8, 4, 16, W), BF16), vm((NJ, 7, 4, 16, W), BF16), vm((NJ, 3, 8, 16, W), BF16),
            vm((NJ, 4, 16, W), F32), vm((NJ, 8, 16, W), F32),
            vm((NJ, 4, 16, W), BF16), vm((NJ, 8, 16, W), BF16),
            vm((NJ, 3, 16, W), BF16), vm((NJ, 7, 16, W), BF16),
            dma((14,)), dma((4, 6)), dma((4, 6)), dma((2, NJ)), dma((2, NJ)), dma((NJ, 6)), dma((NJ, 6)),
            dma((2, NJ, 2)), dma((2, NJ, 2)), dma((2, NJ)), dma((2, NJ)),
            dma((NJ,)), dma((NJ,)), dma((NJ, 4)), dma((NJ, 4)),
        ],
        compiler_params=pltpu.CompilerParams(
            collective_id=0, has_side_effects=True, vmem_limit_bytes=56 * 2**20
        ),
        name="sophia",
    )(acts, targets, probe, master, moment, curv)
    return pl.pallas_call(
        copy_kernel,
        out_shape=shapes,
        in_specs=[vmem_spec] * 3,
        out_specs=(vmem_spec,) * 3,
        name="write_out",
    )(*results)


def solution(mesh):
    in_specs = (
        P("dp", "tensor"),
        P("dp", None),
        P("tensor", None),
        P(("tensor", "dp"), None),
        P(("tensor", "dp"), None),
        P(("tensor", "dp"), None),
    )
    out_specs = (P("tensor", None), P(("tensor", "dp"), None), P(("tensor", "dp"), None))
    return jax.shard_map(body, mesh=mesh, in_specs=in_specs, out_specs=out_specs, check_vma=False)
```

```python
import math

import jax
import jax.numpy as jnp
from jax import lax
from jax.experimental import pallas as pl
from jax.experimental.pallas import tpu as pltpu
from jax.sharding import PartitionSpec as P

MESH = pl.DeviceIdType.MESH
F32 = jnp.float32
BF16 = jnp.bfloat16
NJ = 3
W = 128
A_, B_, C_, D_, E_, F_ = range(6)


def mm(a, b):
    return lax.dot_general(a, b, (((1,), (0,)), ((), ())), preferred_element_type=F32)


def mm_t(a, b):
    return lax.dot_general(a, b, (((1,), (1,)), ((), ())), preferred_element_type=F32)


def kernel(
    acts_hbm, targets_hbm, probe_hbm, master_hbm, moment_hbm, curv_hbm,
    new_hbm, moment_hbm_out, curv_hbm_out,
    master_in, moment_in, curv_in, moment_out, curv_out,
    acts, probe, targets, signs, acts_pad, sel_t,
    master16, moment16, curv16, signs16,
    wbuf, nbuf, sig, obuf,
    s0, r0, s1, r1, keep0, own0, keep1, own1, tot0, tot1, swap_out, swap_in,
    dsend, drecv, town, tsend, recv_a1, recv_b1, sum_a, sum_b, send_a2, send_b2, recv_a2, recv_b2,
    local_sem, rs_ss, rs_rs, sw_ss, sw_rs, ag_ss, ag_rs,
    wa_ss, wa_rs, wc_ss, wc_rs, d_ss, d_rs, t_ss, t_rs,
):
    inverse = 1.0 / math.sqrt(acts_hbm.shape[0] * lax.axis_size("dp"))
    dp = lax.axis_index("dp")
    tensor = lax.axis_index("tensor")
    y, zl, c = dp // 8, (dp // 2) % 4, dp % 2
    zh, x = tensor // 4, tensor % 4
    right, left, opp = (x + 1) % 4, (x + 3) % 4, (x + 2) % 4

    def dev(y_=None, zl_=None, c_=None, zh_=None, x_=None):
        y_ = y if y_ is None else y_
        zl_ = zl if zl_ is None else zl_
        c_ = c if c_ is None else c_
        zh_ = zh if zh_ is None else zh_
        x_ = x if x_ is None else x_
        return (y_ * 8 + zl_ * 2 + c_, zh_ * 4 + x_)

    to_right, to_left = dev(x_=right), dev(x_=left)
    to_zh, to_core = dev(zh_=1 - zh), dev(c_=1 - c)
    to_zl = [dev(zl_=(zl + i) % 4) for i in range(1, 4)]
    to_y = [dev(y_=(y + i) % 8) for i in range(1, 8)]

    own16 = pl.multiple_of(c * 512 + y * 64 + zl * 16, 16)
    own512 = pl.multiple_of(c * 512, 512)

    def rcopy(src, dst, ss, rs, to):
        return pltpu.make_async_remote_copy(
            src_ref=src, dst_ref=dst, send_sem=ss, recv_sem=rs, device_id=to, device_id_type=MESH
        )

    sent, bulk = [], []

    def send(src, dst, sems, to):
        ss, rs, at = sems
        copy = rcopy(src, dst, ss.at[at], rs.at[at], to)
        copy.start()
        sent.append(copy)

    def arrived(dst, rs, at):
        rcopy(dst, dst, rs.at[at], rs.at[at], to_core).wait_recv()

    def rows256(q):
        return pl.ds(pl.multiple_of(q * 256, 256), 256)

    barrier = pltpu.get_barrier_semaphore()
    partners = [to_right, to_left, to_zh, to_core] + to_zl + to_y
    for to in partners:
        pl.semaphore_signal(barrier, inc=1, device_id=to, device_id_type=MESH)

    state_loads = []
    for n, (src, dst) in enumerate(
        ((master_hbm, master_in), (moment_hbm, moment_in), (curv_hbm, curv_in))
    ):
        load = pltpu.make_async_copy(src, dst, local_sem.at[9 + n])
        load.start()
        state_loads.append(load)
    probe_load = pltpu.make_async_copy(probe_hbm, probe, local_sem.at[0])
    probe_load.start()
    act_loads = []
    for n, q in enumerate((opp, right, left, x)):
        load = pltpu.make_async_copy(
            acts_hbm.at[rows256(q), :], acts.at[rows256(q), :], local_sem.at[1 + n]
        )
        load.start()
        act_loads.append(load)
    target_load = pltpu.make_async_copy(targets_hbm.at[rows256(x), :], targets, local_sem.at[5])
    target_load.start()

    def meet():
        pl.semaphore_wait(barrier, len(partners))

    def load_rows():
        state_loads[0].wait()
        master16[...] = jnp.zeros_like(master16)
        master16[0:14, :] = master_in[...]
        low = master16[...].astype(BF16)
        for j in range(NJ):
            wbuf[j, c, y, zl] = low[:, j * W : (j + 1) * W]

    def load_states():
        for n, (padded, ref) in enumerate(((moment16, moment_in), (curv16, curv_in))):
            state_loads[1 + n].wait()
            padded[...] = jnp.zeros_like(padded)
            padded[0:14, :] = ref[...]

    def spread(copies, whole, sems):
        ss, rs, at = sems
        for src, dst, to in copies:
            rcopy(src, dst, ss.at[at], rs.at[at], to).start()
        bulk.append((whole, ss, at))

    def gather_1(buf, k, j):
        own = buf.at[j, c, y, zl]
        peers = to_y if j == 1 else to_zl
        whole = buf.at[j, 0, 0:7, 0] if j == 1 else buf.at[j, 0, 0, 0:3]
        spread([(own, own, to) for to in peers], whole, (wa_ss, wa_rs, (k, j, 0)))

    def gather_2(buf, k, j):
        if j == 1:
            arrived(buf.at[j, 0, 0:7, 0], wa_rs, (k, j, 0))
            block, peers, whole = buf.at[j, c, :, zl], to_zl, buf.at[j, 0, :, 0:3]
        else:
            arrived(buf.at[j, 0, 0, 0:3], wa_rs, (k, j, 0))
            block, peers, whole = buf.at[j, c, y], to_y, buf.at[j, 0, 0:7]
        spread([(block, block, to) for to in peers], whole, (wa_ss, wa_rs, (k, j, 1)))

    def gather_core(buf, k, j):
        whole = buf.at[j, 0, :, 0:3] if j == 1 else buf.at[j, 0, 0:7]
        arrived(whole, wa_rs, (k, j, 1))
        send(buf.at[j, c], buf.at[j, c], (wc_ss, wc_rs, (k, j)), to_core)

    def gathered(buf, k, j):
        arrived(buf.at[j, 0], wc_rs, (k, j))

    def bufs(g):
        if g == 0:
            return s0, r0, keep0, own0, tot0
        return s1.at[g - 1], r1.at[g - 1], keep1.at[g - 1], own1.at[g - 1], tot1.at[g - 1]

    def partial_sum(g, q, load):
        if g == 0:
            load.wait()
            return mm(acts[rows256(q), :], signs[...])
        return mm(acts_pad[rows256(q), :], wbuf[g - 1].reshape(1024, W))

    def reduce_send(g, kind, to):
        sb, rb = bufs(g)[:2]
        send(sb.at[kind], rb.at[kind], (rs_ss, rs_rs, (g, kind,)), to)

    def reduce_got(g, kind):
        rb = bufs(g)[1]
        arrived(rb.at[kind], rs_rs, (g, kind,))

    def reduce_0(g):
        sb = bufs(g)[0]
        part = partial_sum(g, opp, act_loads[0])
        sb[A_] = part[:128].astype(BF16)
        sb[B_] = part[128:].astype(BF16)

    def reduce_1(g):
        sb, rb, keep, own, tot = bufs(g)
        reduce_send(g, A_, to_right)
        reduce_send(g, B_, to_left)
        part = partial_sum(g, right, act_loads[1])
        sb[C_] = part[128:].astype(BF16)
        reduce_send(g, C_, to_right)
        keep[0] = part[:128]
        part = partial_sum(g, left, act_loads[2])
        sb[D_] = part[:128].astype(BF16)
        reduce_send(g, D_, to_left)
        keep[1] = part[128:]
        own[...] = partial_sum(g, x, act_loads[3])

    def reduce_2(g):
        sb, rb, keep, own, tot = bufs(g)
        reduce_got(g, A_)
        sb[E_] = (keep[0] + rb[A_].astype(F32)).astype(BF16)
        reduce_send(g, E_, to_right)
        reduce_got(g, B_)
        sb[F_] = (keep[1] + rb[B_].astype(F32)).astype(BF16)
        reduce_send(g, F_, to_left)

    def reduce_3(g):
        sb, rb, keep, own, tot = bufs(g)
        for kind in (C_, D_, E_, F_):
            reduce_got(g, kind)
        tot[0:128, :] = own[0:128, :] + rb[E_].astype(F32) + rb[D_].astype(F32)
        tot[128:256, :] = own[128:256, :] + rb[C_].astype(F32) + rb[F_].astype(F32)
        if g == 0:
            for j in range(NJ):
                swap_out[0, j] = tot[:, j * W : (j + 1) * W].astype(BF16)
        else:
            swap_out[1, g - 1] = tot[...].astype(BF16)
            swap(1, g - 1)

    def swap(k, j):
        send(swap_out.at[k, j], swap_in.at[k, j], (sw_ss, sw_rs, (k, j)), to_zh)

    def swapped(k, j, own):
        arrived(swap_in.at[k, j], sw_rs, (k, j))
        return own + swap_in[k, j].astype(F32)

    def signal_send(j, q, h, idx, to):
        rows = pl.ds(pl.multiple_of(q * 256 + h * 128, 128), 128)
        send(sig.at[j, rows], sig.at[j, rows], (ag_ss, ag_rs, (j, idx)), to)

    def signal_got(j, idx):
        arrived(sig.at[j, pl.ds(0, 128)], ag_rs, (j, idx))

    def signal_a(j):
        cols = slice(j * W, (j + 1) * W)
        probed = swapped(0, j, tot0[:, cols])
        out = swapped(1, j, tot1[j])
        slope = jnp.tanh(out - targets[:, cols].astype(F32))
        bend = (1.0 - slope * slope) * probed
        sig[j, rows256(x), 0:W] = (slope * inverse).astype(BF16)
        sig[j, rows256(x), W : 2 * W] = (bend * inverse).astype(BF16)
        signal_send(j, x, 0, 0, to_right)
        signal_send(j, x, 1, 3, to_left)
        signal_send(j, x, 1, 1, to_right)
        signal_send(j, x, 0, 2, to_left)

    def signal_c(j):
        signal_got(j, 0)
        signal_send(j, left, 0, 4, to_right)
        signal_got(j, 3)
        signal_send(j, right, 1, 5, to_left)

    def signal_d(j):
        for idx in (1, 2, 4, 5):
            signal_got(j, idx)

    def contract(rows, j):
        return lax.dot_general(
            acts_pad[:, rows], sig[j], (((0,), (0,)), ((), ())), preferred_element_type=F32
        )

    def terms_core(j):
        dsend[j] = contract(pl.ds(pl.multiple_of((1 - c) * 512, 512), 512), j).astype(BF16)
        send(dsend.at[j], drecv.at[j], (d_ss, d_rs, (j,)), to_core)
        town[j] = contract(pl.ds(own512, 512), j).reshape(8, 4, 16, 2 * W)

    def terms_1(j):
        arrived(drecv.at[j], d_rs, (j,))
        total = town[j] + drecv[j].astype(F32).reshape(8, 4, 16, 2 * W)
        town[j] = total
        tsend[j, 0] = total[..., :W].astype(BF16)
        tsend[j, 1] = total[..., W:].astype(BF16)
        spread(
            [(tsend.at[j, 1, :, (zl + 1 + i) % 4], recv_b1.at[j, i], to_zl[i]) for i in range(3)],
            recv_b1.at[j], (t_ss, t_rs, (j, 1)),
        )
        spread(
            [(tsend.at[j, 0, (y + 1 + i) % 8], recv_a1.at[j, i], to_y[i]) for i in range(7)],
            recv_a1.at[j], (t_ss, t_rs, (j, 0)),
        )

    def terms_2a(j):
        arrived(recv_a1.at[j], t_rs, (j, 0))
        total = town[j, y, :, :, 0:W]
        for i in range(7):
            total = total + recv_a1[j, i].astype(F32)
        sum_a[j] = total
        send_a2[j] = total.astype(BF16)
        spread(
            [(send_a2.at[j, (zl + 1 + i) % 4], recv_a2.at[j, i], to_zl[i]) for i in range(3)],
            recv_a2.at[j], (t_ss, t_rs, (j, 2)),
        )

    def terms_2b(j):
        arrived(recv_b1.at[j], t_rs, (j, 1))
        total = town[j, :, zl, :, W : 2 * W]
        for i in range(3):
            total = total + recv_b1[j, i].astype(F32)
        sum_b[j] = total
        send_b2[j] = total.astype(BF16)
        spread(
            [(send_b2.at[j, (y + 1 + i) % 8], recv_b2.at[j, i], to_y[i]) for i in range(7)],
            recv_b2.at[j], (t_ss, t_rs, (j, 3)),
        )

    def update(j):
        arrived(recv_a2.at[j], t_rs, (j, 2))
        grad = sum_a[j, zl]
        for i in range(3):
            grad = grad + recv_a2[j, i].astype(F32)
        arrived(recv_b2.at[j], t_rs, (j, 3))
        hvp = sum_b[j, y]
        for i in range(7):
            hvp = hvp + recv_b2[j, i].astype(F32)
        cols = slice(j * W, (j + 1) * W)
        estimate = signs16[:, cols] * hvp
        moment = 0.9 * moment16[:, cols] + 0.1 * grad
        curv = 0.9 * curv16[:, cols] + 0.1 * estimate
        moment_out[:, cols] = moment[0:14]
        curv_out[:, cols] = curv[0:14]
        step = jnp.clip(moment / jnp.maximum(0.05 * curv, 0.02), -1.0, 1.0)
        master = master16[:, cols]
        updated = master - 0.02 * (step + 0.1 * master)
        real = lax.broadcasted_iota(jnp.int32, updated.shape, 0) < 14
        nbuf[j, c, y, zl] = jnp.where(real, updated, 0.0).astype(BF16)
        gather_1(nbuf, 1, j)

    stores = []

    def store_states():
        for n, (src, dst) in enumerate(((moment_out, moment_hbm_out), (curv_out, curv_hbm_out))):
            store = pltpu.make_async_copy(src, dst, local_sem.at[12 + n])
            store.start()
            stores.append(store)

    def finish(j):
        gathered(nbuf, 1, j)
        obuf[j] = mm(sel_t[...], nbuf[j].reshape(1024, W)).astype(BF16)
        store = pltpu.make_async_copy(
            obuf.at[j], new_hbm.at[:, pl.ds(j * W, W)], local_sem.at[6 + j]
        )
        store.start()
        stores.append(store)

    def source(p):
        r = p % 16
        row = (((p // 64) % 8) * 8 + ((p // 16) % 4) * 2 + p // 512) * 14 + r
        return jnp.where(r < 14, row, -1)

    def make_signs():
        probe_load.wait()
        signs[...] = (2 * probe[...] - 1).astype(F32).astype(BF16)

    def make_sel_t():
        @pl.loop(0, 7)
        def _(t):
            rows = pl.ds(pl.multiple_of(t * 128, 128), 128)
            k = lax.broadcasted_iota(jnp.int32, (128, 1024), 0) + t * 128
            p = source(lax.broadcasted_iota(jnp.int32, (1, 1024), 1))
            sel_t[rows, :] = jnp.where(k == p, 1.0, 0.0).astype(BF16)

    def make_acts_pad(first, last):
        @pl.loop(first, last)
        def _(t):
            rows = pl.ds(pl.multiple_of(t * 256, 256), 256)
            acts_pad[rows, :] = mm(acts[rows, :], sel_t[...]).astype(BF16)

    def make_signs16():
        p = source(lax.broadcasted_iota(jnp.int32, (16, 1), 0) + own16)
        k = lax.broadcasted_iota(jnp.int32, (16, 896), 1)
        signs16[...] = mm(jnp.where(k == p, 1.0, 0.0).astype(BF16), signs[...])

    def all_sent():
        for copy in sent:
            copy.wait_send()
        for ref, ss, at in bulk:
            rcopy(ref, ref, ss.at[at], ss.at[at], to_core).wait_send()
        sent.clear()
        bulk.clear()

    steps = [
        (load_rows,), (meet,), (gather_1, wbuf, 0, 0), (gather_1, wbuf, 0, 1),
        (gather_1, wbuf, 0, 2), (make_signs,), (reduce_0, 0), (reduce_1, 0),
        (gather_2, wbuf, 0, 0), (gather_2, wbuf, 0, 1), (reduce_2, 0), (gather_2, wbuf, 0, 2),
        (make_sel_t,), (make_acts_pad, 0, 4), (gather_core, wbuf, 0, 0), (reduce_3, 0),
        (gather_core, wbuf, 0, 1), (swap, 0, 0), (gathered, wbuf, 0, 0), (reduce_0, 1),
        (reduce_1, 1), (gather_core, wbuf, 0, 2), (gathered, wbuf, 0, 1), (swap, 0, 1),
        (reduce_0, 2), (reduce_1, 2), (reduce_2, 1), (gathered, wbuf, 0, 2), (reduce_2, 2),
        (reduce_3, 1), (reduce_0, 3), (reduce_1, 3), (reduce_3, 2), (swap, 0, 2),
        (reduce_2, 3), (make_signs16,), (load_states,), (target_load.wait,), (reduce_3, 3), (signal_a, 0),
        (signal_a, 1), (signal_c, 0), (signal_c, 1), (signal_a, 2), (signal_d, 0),
        (terms_core, 0), (signal_d, 1), (terms_core, 1), (signal_c, 2), (terms_1, 0),
        (terms_1, 1), (signal_d, 2), (terms_core, 2), (terms_1, 2), (terms_2b, 0),
        (terms_2a, 0), (terms_2b, 1), (terms_2a, 1), (terms_2b, 2), (terms_2a, 2),
        (update, 0), (update, 1), (update, 2), (store_states,), (gather_2, nbuf, 1, 0), (gather_2, nbuf, 1, 1),
        (gather_2, nbuf, 1, 2), (gather_core, nbuf, 1, 0), (gather_core, nbuf, 1, 1),
        (finish, 0), (all_sent,), (gather_core, nbuf, 1, 2), (finish, 1), (finish, 2),
    ]
    for step, *values in steps:
        step(*values)
    for store in stores:
        store.wait()
    all_sent()


def copy_kernel(*refs):
    count = len(refs) // 2
    for n in range(count):
        refs[count + n][...] = refs[n][...]


def body(acts, targets, probe, master, moment, curv):
    any_spec = pl.BlockSpec(memory_space=pl.ANY)
    vmem_spec = pl.BlockSpec(memory_space=pltpu.VMEM)
    dma = pltpu.SemaphoreType.DMA
    vm = pltpu.VMEM
    shapes = (
        jax.ShapeDtypeStruct((896, 384), BF16),
        jax.ShapeDtypeStruct((14, 384), F32),
        jax.ShapeDtypeStruct((14, 384), F32),
    )
    results = pl.pallas_call(
        kernel,
        out_shape=shapes,
        in_specs=[any_spec] * 6,
        out_specs=(any_spec,) * 3,
        scratch_shapes=[
            vm((14, 384), F32), vm((14, 384), F32), vm((14, 384), F32), vm((14, 384), F32),
            vm((14, 384), F32),
            vm((1024, 896), BF16), vm((896, 384), jnp.int32), vm((256, 384), BF16),
            vm((896, 384), BF16), vm((1024, 1024), BF16), vm((896, 1024), BF16),
            vm((16, 384), F32), vm((16, 384), F32), vm((16, 384), F32), vm((16, 384), F32),
            vm((NJ, 2, 8, 4, 16, W), BF16), vm((NJ, 2, 8, 4, 16, W), BF16),
            vm((NJ, 1024, 2 * W), BF16), vm((NJ, 896, W), BF16),
            vm((6, 128, 384), BF16), vm((6, 128, 384), BF16),
            vm((NJ, 6, 128, W), BF16), vm((NJ, 6, 128, W), BF16),
            vm((2, 128, 384), F32), vm((256, 384), F32),
            vm((NJ, 2, 128, W), F32), vm((NJ, 256, W), F32),
            vm((256, 384), F32), vm((NJ, 256, W), F32),
            vm((2, NJ, 256, W), BF16), vm((2, NJ, 256, W), BF16),
            vm((NJ, 512, 2 * W), BF16), vm((NJ, 512, 2 * W), BF16), vm((NJ, 8, 4, 16, 2 * W), F32),
            vm((NJ, 2, 8, 4, 16, W), BF16), vm((NJ, 7, 4, 16, W), BF16), vm((NJ, 3, 8, 16, W), BF16),
            vm((NJ, 4, 16, W), F32), vm((NJ, 8, 16, W), F32),
            vm((NJ, 4, 16, W), BF16), vm((NJ, 8, 16, W), BF16),
            vm((NJ, 3, 16, W), BF16), vm((NJ, 7, 16, W), BF16),
            dma((14,)), dma((4, 6)), dma((4, 6)), dma((2, NJ)), dma((2, NJ)), dma((NJ, 6)), dma((NJ, 6)),
            dma((2, NJ, 2)), dma((2, NJ, 2)), dma((2, NJ)), dma((2, NJ)),
            dma((NJ,)), dma((NJ,)), dma((NJ, 4)), dma((NJ, 4)),
        ],
        compiler_params=pltpu.CompilerParams(
            collective_id=0, has_side_effects=True, vmem_limit_bytes=56 * 2**20
        ),
        name="sophia",
    )(acts, targets, probe, master, moment, curv)
    return pl.pallas_call(
        copy_kernel,
        out_shape=shapes,
        in_specs=[vmem_spec] * 3,
        out_specs=(vmem_spec,) * 3,
        name="write_out",
    )(*results)


def solution(mesh):
    in_specs = (
        P("dp", "tensor"),
        P("dp", None),
        P("tensor", None),
        P(("tensor", "dp"), None),
        P(("tensor", "dp"), None),
        P(("tensor", "dp"), None),
    )
    out_specs = (P("tensor", None), P(("tensor", "dp"), None), P(("tensor", "dp"), None))
    return jax.shard_map(body, mesh=mesh, in_specs=in_specs, out_specs=out_specs, check_vma=False)
```
